128 devices in a mesh: kb: 16 (over y, z), col: 8 (over x, core).
Axes of the slice: x: 4, y: 4, z: 4, core: 2. Of those that a mesh axis runs over, the one named last changes fastest.
Arguments:
- q_index: int32 [16384, 1], P(('kb', 'col')), may hold values from 0 to 127; in each aligned block of 128 rows (0 to 127, 128 to 255, ...) at most 2 rows name the same one
- cond_pairs: bfloat16 [16384, 16, 1200], P(('kb', 'col')), may hold values from -1 to 1
- val_pairs: bfloat16 [16384, 16, 1200], P(('kb', 'col')), may hold values from -1 to 1
- row_vc: bfloat16 [256, 16, 1200], P(('kb', 'col')), may hold values from -1 to 1
- col_vc: bfloat16 [64, 16, 1200], P('col'), may hold values from -1 to 1
- coulomb: float32 [1200], replicated, may hold values from 0.1 to 3
- screened: bfloat16 [128, 1200, 1200], P(('kb', 'col')), may hold values from -0.1875 to 0.1875
Outputs:
- kernel: float32 [16384, 256], P(('kb', 'col'))
The draws below stay inside these ranges and needn't reach their ends.
Inputs may be any that keep to these rules, and one draw needn't show every extreme that they name: `q_index`: among the 128 pairs of one device (aligned blocks of rows) no momentum transfer occurs more than 2 times, a bound that some block reaches; every momentum transfer occurs somewhere.
All inputs are finite; a program needn't handle non-finite values.
Results may differ from the reference program's by a relative error of at most 0.0029.
Values may be sent and summed in bfloat16 or wider, within the bound.
A program may use at most 192 MiB of HBM per device.

```python
import math
import jax
import jax.numpy as jnp
import numpy as np
from jax import lax

G = 1200
NV = 4
NC = 4
KR_DEV = 16
KC_DEV = 8
P_DEV = 128
PAIRS = 16384
KROWS = 256
KCOLS = 64
Q = 128
MOST = 2
N_KB = 16
N_COL = 8


def shard_levels(key, dims, split, smallest, high):
    def one(axis_at, parts):
        draws = jax.random.uniform(jax.random.fold_in(jax.random.fold_in(key, 6), axis_at), (parts,), jnp.float32, smallest / len(split), high / len(split))
        return jnp.repeat(jnp.exp(draws), dims[axis_at] // parts).reshape((-1,) + (1,) * (len(dims) - axis_at - 1))

    level = one(*split[0])
    for cut in split[1:]:
        level = level * one(*cut)
    return level


def assign_block(stream_key, own, number, rows, number_of, top, reach, lean):
    sequence = jax.random.permutation(stream_key, number_of)
    packed, ordinary = load_shares(number_of, rows * top, reach, lean, True), load_shares(number_of, rows * top, reach, lean, False)
    places = jnp.arange(number_of)

    def named(sizes, offset_by):
        used = int((sizes > 0).sum())
        fixed = max(1, used // 4)
        moved = fixed + (places - fixed + offset_by * (used - fixed)) % max(1, number_of - fixed)
        return jnp.zeros((number_of,), jnp.int32).at[sequence[jnp.where(places < fixed, places, moved)]].set(jnp.asarray(sizes, jnp.int32))

    sizes = jnp.where(number % 4 == 0, named(packed, number // 4), named(ordinary, number - number // 4 - 1))
    mixed = jax.random.permutation(jax.random.fold_in(own, 3), number_of)
    giver, sink = mixed[0:number_of // 2 * 2:2], mixed[1:number_of // 2 * 2:2]
    margin = jnp.minimum(sizes[giver] - 1, reach - sizes[sink]) // 2
    margin = jnp.where((giver == sequence[0]) | (sink == sequence[0]) | (sizes[sink] == 0), 0, jnp.maximum(margin, 0))
    moved = jax.random.randint(jax.random.fold_in(own, 4), (number_of // 2,), 0, 1 << 20) % (margin + 1)
    sizes = sizes.at[giver].add(-moved).at[sink].add(moved)
    items = jnp.searchsorted(jnp.cumsum(sizes), jnp.arange(rows * top), side="right").astype(jnp.int32)
    listing = items.reshape(top, rows).T
    listing = listing[jax.random.permutation(jax.random.fold_in(own, 1), rows)]
    offset_by = jax.random.randint(jax.random.fold_in(own, 2), (rows, 1), 0, top)
    return jnp.take_along_axis(listing, (jnp.arange(top)[None, :] + offset_by) % top, axis=1)


def load_shares(number_of, total, bound, slope, full):
    portions = [(1 << 20) // math.isqrt(grade ** slope) + 1 for grade in range(1, number_of + 1)]
    largest = bound if full else min(bound, max(-(-total // number_of), total * portions[0] // sum(portions)))
    least = 1 if total - largest >= number_of - 1 else 0
    given, spare = [largest] + [least] * (number_of - 1), total - largest - least * (number_of - 1)
    while spare > 0:
        free = [i for i in range(1, number_of) if given[i] < largest] or [i for i in range(1, number_of) if given[i] < bound]
        pool, budget = sum([portions[i] for i in free]), spare
        for i in free:
            addition = min(bound - given[i], max(1, budget * portions[i] // pool), spare)
            given[i] = given[i] + addition
            spare = spare - addition
    return np.array(given)


def centred(stream_key, extent, spread, limit, shards=(), kind=jnp.bfloat16):
    values = spread * jax.random.normal(stream_key, extent, jnp.float32)
    if shards:
        values = values * shard_levels(stream_key, extent, shards, -0.22, 0.18)
    return jnp.clip(values, -limit, limit).astype(kind)


def setup_inputs(seed: int = 0) -> dict:
    seeds = jax.random.split(jax.random.key(seed), 8)
    q_index_keys = jax.random.split(jax.random.fold_in(seeds[0], 1), PAIRS // P_DEV)
    q_index_turns = jax.random.permutation(jax.random.fold_in(seeds[0], 3), PAIRS // P_DEV)
    q_index = jax.vmap(lambda own, number: assign_block(jax.random.fold_in(seeds[0], 2), own, number, P_DEV, Q, 1, MOST, 2))(q_index_keys, q_index_turns).reshape((PAIRS, 1))
    cond_pairs = centred(seeds[1], (PAIRS, NC * NC, G), 0.17, 1.0, ((0, 128),))
    val_pairs = centred(seeds[2], (PAIRS, NV * NV, G), 0.17, 1.0, ((0, 128),))
    row_vc = centred(seeds[3], (KROWS, NV * NC, G), 0.17, 1.0, ((0, 128),))
    col_vc = centred(seeds[4], (KCOLS, NV * NC, G), 0.17, 1.0, ((0, 8),))
    coulomb = jnp.clip(jnp.exp(jax.random.uniform(seeds[5], (G,), jnp.float32, math.log(0.1), math.log(3.0))), 0.1, 3.0)
    screened = centred(seeds[6], (Q, G, G), G ** -0.5, 0.1875, ((0, 128),))
    return dict(q_index=q_index, cond_pairs=cond_pairs, val_pairs=val_pairs, row_vc=row_vc, col_vc=col_vc, coulomb=coulomb, screened=screened)


def reference(q_index, cond_pairs, val_pairs, row_vc, col_vc, coulomb, screened):
    def direct_one(items):
        mcc, mvv, qq = items
        wmat = lax.dynamic_index_in_dim(screened, qq, 0, keepdims=False)
        applied = jnp.dot(mvv, wmat.T, preferred_element_type=jnp.float32).astype(jnp.bfloat16)
        return jnp.dot(mcc, applied.T, preferred_element_type=jnp.float32).reshape(NC * NC * NV * NV)

    direct = lax.map(direct_one, (cond_pairs, val_pairs, q_index[:, 0].astype(jnp.int32)))
    direct = direct.reshape(PAIRS, NC, NC, NV, NV).transpose(0, 3, 1, 4, 2).reshape(PAIRS, NV * NC * NV * NC)
    scaled = (col_vc.astype(jnp.float32) * coulomb[None, None, :]).astype(jnp.bfloat16)
    full = jnp.einsum('avg,bwg->abvw', row_vc.astype(jnp.float32), scaled.astype(jnp.float32))
    full = full.reshape(N_KB, KR_DEV, N_COL, KC_DEV, NV * NC * NV * NC)
    exchange = full.transpose(0, 2, 1, 3, 4).reshape(PAIRS, NV * NC * NV * NC)
    return 2.0 * exchange - direct
```

```python
import functools

import jax
import jax.numpy as jnp
from jax import lax
from jax.experimental import pallas as pl
from jax.experimental.pallas import tpu as pltpu
from jax.sharding import PartitionSpec as P

MESH = pl.DeviceIdType.MESH
Z, Y, X = 0, 1, 2
ORDERS = ((X, Y, Z), (Y, Z, X), (Z, X, Y))
SLOTS = 4
MAIN = 1152
WIDE = 1280


def streams(cols):
    third = 384
    cuts = (0, third, 2 * third, cols)
    out = [(j, ORDERS[j], 0, cols) for j in range(3)]
    return out + [(3, ORDERS[i], cuts[i], cuts[i + 1]) for i in range(3)]


def at_axis(ref, lead, axis, index, c0, c1):
    where = [slice(None)] * 3
    where[axis] = index
    return ref.at[(lead, *where, slice(None), slice(c0, c1))]


def place_kernel(
    tab, val_hbm, cond_hbm, tail_ref, w_hbm,
    out_ref, r1v, r2v, r1c, r2c,
    vin, sv, sc, fv, fc, w2, tt, zbuf, dbuf,
    in_sem, w_sem, send, recv, last, local, back_send, back_recv,
):
    kb = lax.axis_index("kb")
    col = lax.axis_index("col")
    here = (kb & 3, kb >> 2, col >> 1)
    core = col & 1
    n_dev = 128

    def dev(chip, which):
        return (chip[Y] * 4 + chip[Z], chip[X] * 2 + which)

    def moved(axis, index):
        chip = list(here)
        chip[axis] = index
        return tuple(chip)

    barrier = pltpu.get_barrier_semaphore()
    me = kb * 8 + col

    load_val = pltpu.make_async_copy(val_hbm, vin, in_sem.at[0])
    load_val.start()
    load_w = pltpu.make_async_copy(w_hbm, w2.at[core], in_sem.at[1])
    load_w.start()

    @pl.loop(1, n_dev)
    def _(k):
        t = me ^ k
        pl.semaphore_signal(barrier, inc=1, device_id=(t >> 3, t & 7), device_id_type=MESH)

    load_val.wait()

    @pl.loop(0, 64)
    def _(chip):
        z, y, x = chip >> 4, (chip >> 2) & 3, chip & 3
        for j in range(SLOTS):
            p = tab[j * 64 + chip]
            sv[j, z, y, x, :, :MAIN] = vin[p, :, :MAIN]
            sv[j, z, y, x, :, MAIN:] = tail_ref[p]

    pl.semaphore_wait(barrier, n_dev - 1)
    load_cond = pltpu.make_async_copy(cond_hbm, vin, in_sem.at[0])
    load_cond.start()
    send_w = pltpu.make_async_remote_copy(
        w_hbm, w2.at[core], w_sem.at[0], w_sem.at[1], device_id=dev(here, 1 - core), device_id_type=MESH
    )
    send_w.start()

    rounds = ((sv, r1v, r2v, fv), (sc, r1c, r2c, fc))
    parts = (streams(WIDE), streams(MAIN))

    def ring(r, s, k, d):
        j, order, c0, c1 = parts[r][s]
        axis = order[k]
        src, dst = rounds[r][k], rounds[r][k + 1]
        there = (here[axis] + d) & 3
        return pltpu.make_async_remote_copy(
            at_axis(src, j, axis, there, c0, c1),
            at_axis(dst, j, axis, here[axis], c0, c1),
            send.at[r, s, k, d], recv.at[r, s, k, d],
            device_id=dev(moved(axis, there), core), device_id_type=MESH,
        )

    def keep(r, s, k):
        j, order, c0, c1 = parts[r][s]
        axis = order[k]
        return pltpu.make_async_copy(
            at_axis(rounds[r][k], j, axis, here[axis], c0, c1),
            at_axis(rounds[r][k + 1], j, axis, here[axis], c0, c1),
            local.at[r, s, k],
        )

    def start_ring(r, k):
        for s in range(6):
            keep(r, s, k).start()
        for d in (1, 3, 2):
            for s in range(6):
                ring(r, s, k, d).start()

    def wait_ring(r, k):
        for s in range(6):
            for d in (1, 3, 2):
                c = ring(r, s, k, d)
                c.wait_send()
                c.wait_recv()
            keep(r, s, k).wait()

    def final(r, s, d):
        j, order, c0, c1 = parts[r][s]
        axis = order[2]
        there = (here[axis] + d) & 3
        lead, goal = (core, j) if j < 2 else (j, core)
        src = at_axis(rounds[r][2], j, axis, there, c0, c1)
        dst = at_axis(rounds[r][3], lead, axis, here[axis], c0, c1)
        sem = last.at[r, lead, d] if j < 2 else last.at[r, s, d]
        return pltpu.make_async_remote_copy(
            src, dst, send.at[r, s, 2, d], sem,
            device_id=dev(moved(axis, there), goal), device_id_type=MESH,
        )

    def final_local(r, s):
        j, order, c0, c1 = parts[r][s]
        axis = order[2]
        lead = core if j < 2 else j
        return pltpu.make_async_copy(
            at_axis(rounds[r][2], j, axis, here[axis], c0, c1),
            at_axis(rounds[r][3], lead, axis, here[axis], c0, c1),
            local.at[r, s, 2],
        )

    def start_final(r):
        for s in range(6):
            if s < 2:
                @pl.when(core == s)
                def _():
                    final_local(r, s).start()

                @pl.when(core != s)
                def _():
                    final(r, s, 0).start()
            else:
                final_local(r, s).start()
        for d in (1, 3, 2):
            for s in range(6):
                final(r, s, d).start()

    def wait_final(r):
        for s in range(6):
            for d in (1, 3, 2):
                final(r, s, d).wait_send()
            if s < 2:
                @pl.when(core == s)
                def _():
                    final_local(r, s).wait()

                @pl.when(core != s)
                def _():
                    final(r, s, 0).wait_send()
            else:
                final_local(r, s).wait()
                for d in (1, 3, 2):
                    final(r, s, d).wait_recv()
        for mine in range(2):
            axis = ORDERS[mine][2]

            @pl.when(core == mine)
            def _():
                for lead in range(2):
                    for d in (1, 3, 2) if lead == mine else (1, 3, 2, 0):
                        at = at_axis(rounds[r][3], lead, axis, here[axis], 0, parts[r][0][3])
                        pltpu.make_async_remote_copy(
                            at, at, send.at[r, mine, 2, d], last.at[r, lead, d],
                            device_id=dev(here, 1 - core), device_id_type=MESH,
                        ).wait_recv()

    start_ring(0, 0)
    load_cond.wait()

    @pl.loop(0, 64)
    def _(chip):
        z, y, x = chip >> 4, (chip >> 2) & 3, chip & 3
        for j in range(SLOTS):
            p = tab[j * 64 + chip]
            sc[j, z, y, x] = vin[p, :, :MAIN]

    start_ring(1, 0)
    wait_ring(0, 0)
    start_ring(0, 1)
    wait_ring(1, 0)
    start_ring(1, 1)
    wait_ring(0, 1)
    start_final(0)
    load_w.wait()
    send_w.wait()
    wait_ring(1, 1)
    start_final(1)
    wait_final(0)

    group = lax.broadcasted_iota(jnp.int32, (16, 256), 1) >> 4
    row = lax.broadcasted_iota(jnp.int32, (16, 256), 0)
    nt = (((1,), (1,)), ((), ()))

    def diagonal(full):
        total = jnp.zeros((16, 256), jnp.float32)
        for i in range(16):
            total = jnp.where(group == i, full[16 * i : 16 * i + 16], total)
        return total

    @pl.loop(0, 16)
    def _(i):
        b, z = i >> 2, i & 3
        which = jnp.where(b < 2, core, b - 2)
        x = fv[b, z].reshape(256, WIDE)
        for n in range(5):
            w = w2[which, n * 256 : n * 256 + 256, :]
            part = lax.dot_general(x, w, nt, preferred_element_type=jnp.float32).astype(jnp.bfloat16)
            sv[b, z, :, :, :, n * 256 : n * 256 + 256] = part.reshape(4, 4, 16, 256)
            if n == 4:
                full = lax.dot_general(x[:, MAIN:], part[:, 128:], nt, preferred_element_type=jnp.float32)
                tt[b, z] = diagonal(full)

    wait_final(1)

    @pl.loop(0, 16)
    def _(i):
        b, z = i >> 2, i & 3
        full = lax.dot_general(
            fc[b, z].reshape(256, MAIN),
            sv[b, z, :, :, :, :MAIN].reshape(256, MAIN),
            nt,
            preferred_element_type=jnp.float32,
        )
        got = diagonal(full) + tt[b, z]
        turned = jnp.where(group == row, got, 0.0)
        for k in range(1, 16):
            shifted = pltpu.roll(pltpu.roll(got, 16 - k, 0), 16 * k, 1)
            turned = jnp.where(group == ((row + k) & 15), shifted, turned)
        for slot in range(16):
            zbuf[b, z, slot >> 2, slot & 3, 0:1] = turned[slot : slot + 1, :128]
            zbuf[b, z, slot >> 2, slot & 3, 1:2] = turned[slot : slot + 1, 128:]
        back_core = jnp.where(b < 2, b, core)
        back_slot = jnp.where(b < 2, core, b)

        @pl.loop(0, 16)
        def _(slot):
            y, x = slot >> 2, slot & 3
            mine = (z == here[Z]) & (y == here[Y]) & (x == here[X]) & (back_core == core)
            src = zbuf.at[b, z, y, x]
            dst = dbuf.at[back_slot, here[Z], here[Y], here[X]]

            @pl.when(mine)
            def _():
                pltpu.make_async_copy(src, dst, back_recv).start()

            @pl.when(jnp.logical_not(mine))
            def _():
                pltpu.make_async_remote_copy(
                    src, dst, back_send, back_recv,
                    device_id=dev((z, y, x), back_core), device_id_type=MESH,
                ).start()

    spot = zbuf.at[0, 0, 0, 0]

    @pl.loop(0, 64 * SLOTS - (SLOTS - 1))
    def _(_):
        pltpu.make_async_copy(spot, spot, back_send).wait()

    pltpu.make_async_copy(dbuf, dbuf, back_recv).wait()
    out_ref[...] = dbuf[...]


def direct_terms(tab, val_pairs, cond_pairs, tails, w_pad):
    any_spec = pl.BlockSpec(memory_space=pl.ANY)
    wide = (SLOTS, 4, 4, 4, 16, WIDE)
    main = (SLOTS, 4, 4, 4, 16, MAIN)
    bf16 = jnp.bfloat16
    small = (SLOTS, 4, 4, 4, 2, 128)
    out = pl.pallas_call(
        place_kernel,
        out_shape=(
            jax.ShapeDtypeStruct(small, jnp.float32),
            jax.ShapeDtypeStruct(wide, bf16),
            jax.ShapeDtypeStruct(wide, bf16),
            jax.ShapeDtypeStruct(main, bf16),
            jax.ShapeDtypeStruct(main, bf16),
        ),
        in_specs=[
            pl.BlockSpec(memory_space=pltpu.SMEM),
            any_spec,
            any_spec,
            pl.BlockSpec(memory_space=pltpu.VMEM),
            any_spec,
        ],
        out_specs=(pl.BlockSpec(memory_space=pltpu.VMEM), any_spec, any_spec, any_spec, any_spec),
        scratch_shapes=[
            pltpu.VMEM(val_pairs.shape, bf16),
            pltpu.VMEM(wide, bf16),
            pltpu.VMEM(main, bf16),
            pltpu.VMEM(wide, bf16),
            pltpu.VMEM(main, bf16),
            pltpu.VMEM((2, WIDE, WIDE), bf16),
            pltpu.VMEM((SLOTS, 4, 16, 256), jnp.float32),
            pltpu.VMEM(small, jnp.float32),
            pltpu.VMEM(small, jnp.float32),
            pltpu.SemaphoreType.DMA((2,)),
            pltpu.SemaphoreType.DMA((2,)),
            pltpu.SemaphoreType.DMA((2, 6, 3, 4)),
            pltpu.SemaphoreType.DMA((2, 6, 2, 4)),
            pltpu.SemaphoreType.DMA((2, 6, 4)),
            pltpu.SemaphoreType.DMA((2, 6, 3)),
            pltpu.SemaphoreType.DMA,
            pltpu.SemaphoreType.DMA,
        ],
        compiler_params=pltpu.CompilerParams(
            collective_id=0, has_side_effects=True, vmem_limit_bytes=60 * 2**20
        ),
    )(tab, val_pairs, cond_pairs, tails, w_pad)
    return out[0].reshape(SLOTS * 64, 256)


def shards(q_index, cond_pairs, val_pairs, row_vc, col_vc, coulomb, screened):
    count = cond_pairs.shape[0]
    target = q_index[:, 0]
    same = target[:, None] == target[None, :]
    earlier = jnp.arange(count)[None, :] < jnp.arange(count)[:, None]
    rank = jnp.sum((same & earlier).astype(jnp.int32), axis=1)
    core, x, z, y = target & 1, (target >> 1) & 3, (target >> 3) & 3, (target >> 5) & 3
    place = (rank * 2 + core) * 64 + (z * 4 + y) * 4 + x
    spots = jnp.arange(SLOTS * 64, dtype=jnp.int32)
    tab = jnp.sum(
        jnp.where(place[None, :] == spots[:, None], jnp.arange(count, dtype=jnp.int32)[None, :], 0), axis=1
    )
    gap = jnp.zeros((count, 16, 16), jnp.bfloat16)
    tails = jnp.concatenate([val_pairs[:, :, MAIN:], gap, cond_pairs[:, :, MAIN:], gap], axis=2)
    w = jnp.pad(screened[0], ((0, 0), (0, WIDE - screened.shape[2])))
    w_pad = jnp.concatenate(
        [w[:MAIN], jnp.zeros((64, WIDE), jnp.bfloat16), w[MAIN:], jnp.zeros((16, WIDE), jnp.bfloat16)], axis=0
    )
    direct = direct_terms(tab, val_pairs, cond_pairs, tails, w_pad)[place]
    direct = direct.reshape(count, 4, 4, 4, 4).transpose(0, 3, 1, 4, 2).reshape(count, 256)
    scaled = (col_vc.astype(jnp.float32) * coulomb[None, None, :]).astype(jnp.bfloat16)
    exchange = jnp.einsum(
        "avg,bwg->abvw",
        lax.all_gather(row_vc, "col", axis=0, tiled=True),
        scaled,
        preferred_element_type=jnp.float32,
    )
    return 2.0 * exchange.reshape(count, 256) - direct


def solution(mesh):
    return jax.shard_map(
        shards,
        mesh=mesh,
        in_specs=(
            P(("kb", "col"), None),
            P(("kb", "col"), None, None),
            P(("kb", "col"), None, None),
            P(("kb", "col"), None, None),
            P("col", None, None),
            P(),
            P(("kb", "col"), None, None),
        ),
        out_specs=P(("kb", "col"), None),
        check_vma=False,
    )
```

```python
import functools

import jax
import jax.numpy as jnp
from jax import lax
from jax.experimental import pallas as pl
from jax.experimental.pallas import tpu as pltpu
from jax.sharding import PartitionSpec as P

MESH = pl.DeviceIdType.MESH
Z, Y, X = 0, 1, 2
ORDERS = ((X, Y, Z), (Y, Z, X), (Z, X, Y))
MAIN = 1152
TILE = 128
WIDTHS = (640, 640, 640, 512)
CUTS = ((0, 256, 512, 640), (0, 128, 384, 640), (0, 256, 384, 640), (0, 128, 256, 512))
NT = (((1,), (1,)), ((), ()))


def streams(slots, r):
    out = [(j, ORDERS[j], 0, WIDTHS[r]) for j in range(3)]
    if slots == 4:
        out += [(3, ORDERS[i], CUTS[r][i], CUTS[r][i + 1]) for i in range(3)]
    return out


def at_axis(ref, lead, axis, index, c0=None, c1=None):
    where = [slice(None)] * 3
    where[axis] = index
    return ref.at[(lead, *where, slice(None), slice(c0, c1))]


def place_kernel(
    slots,
    onehot, flag_ref, rows_hbm, cols_ref, coulomb_ref, val_hbm, cond_hbm, w_hbm,
    out_ref, ex_ref, h10, h11, h12, h13, h20, h21, h22, h23,
    vt, ct, s0, s1, s2, s3, f0, f1, f2, f3, w2, wt, st, rows, tt, zbuf, ybuf, xbuf, dbuf,
    in_sem, w_sem, row_sem, send, recv, last, local, back_send, back_recv,
):
    kb = lax.axis_index("kb")
    col = lax.axis_index("col")
    here = (kb & 3, kb >> 2, col >> 1)
    core = col & 1
    count = onehot.shape[0]
    per = 64 * 16

    def dev(chip, which):
        return (chip[Y] * 4 + chip[Z], chip[X] * 2 + which)

    def moved(axis, index):
        chip = list(here)
        chip[axis] = index
        return tuple(chip)

    load_val = pltpu.make_async_copy(val_hbm, vt, in_sem.at[0])
    load_val.start()
    load_tail = pltpu.make_async_copy(cond_hbm.at[:, MAIN:], ct, in_sem.at[1])
    load_tail.start()
    load_w = pltpu.make_async_copy(w_hbm.at[0], w2.at[core], in_sem.at[2])
    load_w.start()
    load_rows = pltpu.make_async_copy(rows_hbm, rows.at[col], in_sem.at[3])
    load_rows.start()

    barrier = pltpu.get_barrier_semaphore()
    for axis in range(3):
        for d in (1, 2, 3):
            for which in range(2):
                pl.semaphore_signal(
                    barrier, inc=1, device_id=dev(moved(axis, (here[axis] + d) & 3), which), device_id_type=MESH
                )
    pl.semaphore_signal(barrier, inc=1, device_id=dev(here, 1 - core), device_id_type=MESH)

    rounds = ((s0, h10, h20, f0), (s1, h11, h21, f1), (s2, h12, h22, f2), (s3, h13, h23, f3))
    parts = tuple(streams(slots, r) for r in range(4))
    n_streams = len(parts[0])

    def fill(buf, tile, chunk_of):
        for row in range(16):
            st[pl.ds(row, count, stride=16), :] = lax.dot_general(
                onehot[...], chunk_of(row), NT, preferred_element_type=jnp.float32
            )
        for j in range(slots):
            buf[j, :, :, :, :, pl.ds(pl.multiple_of(tile * TILE, TILE), TILE)] = (
                st[j * per : (j + 1) * per].astype(jnp.bfloat16).reshape(4, 4, 4, 16, TILE)
            )

    def build(buf, first, tiles):
        @pl.loop(0, tiles)
        def _(t):
            fill(buf, t, lambda row: vt[row, pl.ds(pl.multiple_of((first + t) * TILE, TILE), TILE), :])

    def ring(r, s, k, d):
        j, order, c0, c1 = parts[r][s]
        axis = order[k]
        there = (here[axis] + d) & 3
        return pltpu.make_async_remote_copy(
            at_axis(rounds[r][k], j, axis, there, c0, c1),
            at_axis(rounds[r][k + 1], j, axis, here[axis], c0, c1),
            send.at[r, s, k, d], recv.at[r, s, k, d],
            device_id=dev(moved(axis, there), core), device_id_type=MESH,
        )

    def keep(r, s, k):
        j, order, c0, c1 = parts[r][s]
        axis = order[k]
        return pltpu.make_async_copy(
            at_axis(rounds[r][k], j, axis, here[axis], c0, c1),
            at_axis(rounds[r][k + 1], j, axis, here[axis], c0, c1),
            local.at[r, s, k],
        )

    def start_ring(r, k):
        for d in (1, 3, 2):
            for s in range(n_streams):
                ring(r, s, k, d).start()
        for s in range(n_streams):
            keep(r, s, k).start()

    def wait_ring(r, k):
        for s in range(n_streams):
            for d in (1, 3, 2):
                c = ring(r, s, k, d)
                c.wait_send()
                c.wait_recv()
            keep(r, s, k).wait()

    def final(r, s, d):
        j, order, c0, c1 = parts[r][s]
        axis = order[2]
        there = (here[axis] + d) & 3
        lead, goal = (core, j) if j < 2 else (j, core)
        sem = last.at[r, lead, d] if j < 2 else last.at[r, s, d]
        return pltpu.make_async_remote_copy(
            at_axis(rounds[r][2], j, axis, there, c0, c1),
            at_axis(rounds[r][3], lead, axis, here[axis], c0, c1),
            send.at[r, s, 2, d], sem,
            device_id=dev(moved(axis, there), goal), device_id_type=MESH,
        )

    def final_local(r, s):
        j, order, c0, c1 = parts[r][s]
        axis = order[2]
        lead = core if j < 2 else j
        return pltpu.make_async_copy(
            at_axis(rounds[r][2], j, axis, here[axis], c0, c1),
            at_axis(rounds[r][3], lead, axis, here[axis], c0, c1),
            local.at[r, s, 2],
        )

    def start_final(r):
        for d in (1, 3, 2):
            for s in range(n_streams):
                final(r, s, d).start()
        for s in range(n_streams):
            if s < 2:
                @pl.when(core == s)
                def _():
                    final_local(r, s).start()

                @pl.when(core != s)
                def _():
                    final(r, s, 0).start()
            else:
                final_local(r, s).start()

    def wait_final(r):
        for s in range(n_streams):
            for d in (1, 3, 2):
                final(r, s, d).wait_send()
            if s < 2:
                @pl.when(core == s)
                def _():
                    final_local(r, s).wait()

                @pl.when(core != s)
                def _():
                    final(r, s, 0).wait_send()
            else:
                final_local(r, s).wait()
                for d in (1, 3, 2):
                    final(r, s, d).wait_recv()
        for mine in range(2):
            axis = ORDERS[mine][2]

            @pl.when(core == mine)
            def _():
                for lead in range(2):
                    for d in (1, 3, 2) if lead == mine else (1, 3, 2, 0):
                        at = at_axis(rounds[r][3], lead, axis, here[axis])
                        pltpu.make_async_remote_copy(
                            at, at, send.at[r, mine, 2, d], last.at[r, lead, d],
                            device_id=dev(here, 1 - core), device_id_type=MESH,
                        ).wait_recv()

    load_val.wait()
    build(s0, 0, 5)
    pl.semaphore_wait(barrier, 19)
    start_ring(0, 0)
    load_tail.wait()
    build(s1, 5, 4)
    gap = jnp.zeros((16, TILE), jnp.bfloat16)
    fill(s1, 4, lambda row: jnp.concatenate([vt[row, MAIN:, :], gap, ct[row], flag_ref[...]], axis=0))
    load_cond = pltpu.make_async_copy(cond_hbm, vt, in_sem.at[0])
    load_cond.start()
    start_ring(1, 0)

    send_w = pltpu.make_async_remote_copy(
        w_hbm.at[0], w2.at[core], w_sem.at[0], w_sem.at[1], device_id=dev(here, 1 - core), device_id_type=MESH
    )
    send_w.start()

    def row_copy(d):
        to = lax.rem(col + d, 8)
        return pltpu.make_async_remote_copy(
            rows_hbm, rows.at[col], row_sem.at[0, d], row_sem.at[1, d], device_id=(kb, to), device_id_type=MESH
        )

    for d in range(1, 8):
        row_copy(d).start()

    load_cond.wait()
    build(s2, 0, 5)
    wait_ring(0, 0)
    start_ring(0, 1)
    start_ring(2, 0)
    build(s3, 5, 4)
    wait_ring(1, 0)
    start_ring(1, 1)
    start_ring(3, 0)

    load_rows.wait()
    for d in range(1, 8):
        row_copy(d).wait()
    scaled = (cols_ref[...].astype(jnp.float32) * coulomb_ref[...][None]).astype(jnp.bfloat16)
    ex_ref[...] = lax.dot_general(
        rows[...].reshape(256, 1200), scaled.reshape(128, 1200), NT, preferred_element_type=jnp.float32
    )
    load_w.wait()
    send_w.wait()
    wt[...] = jnp.zeros_like(wt)
    for which in range(2):
        wt[which, 64:112] = w2[which, MAIN:]

    wait_ring(0, 1)
    start_final(0)
    wait_ring(2, 0)
    start_ring(2, 1)
    wait_ring(1, 1)
    start_final(1)
    wait_ring(3, 0)
    start_ring(3, 1)
    wait_ring(2, 1)
    start_final(2)
    wait_final(0)
    wait_ring(3, 1)
    start_final(3)
    wait_final(1)

    group = lax.broadcasted_iota(jnp.int32, (16, 256), 1) >> 4
    line = lax.broadcasted_iota(jnp.int32, (16, 256), 0)

    def diagonal(full):
        total = jnp.zeros((16, 256), jnp.float32)
        for i in range(16):
            total = jnp.where(group == i, full[16 * i : 16 * i + 16], total)
        return total

    def apply(i, times):
        b, z = i >> 2, i & 3
        tail = f1[b, z].reshape(256, 640)
        x = jnp.concatenate([f0[b, z].reshape(256, 640), tail], axis=1)[:, :1200]
        for n, (g0, size) in enumerate(((0, 256), (256, 256), (512, 128), (640, 256), (896, 256), (0, 0))):
            part = times(b, x, tail, g0, size).astype(jnp.bfloat16)
            if size == 0:
                s1[b, z, :, :, :, 512:640] = part.reshape(4, 4, 16, 128)
                tt[b, z] = diagonal(lax.dot_general(tail[:, 512:], part, NT, preferred_element_type=jnp.float32))
            else:
                to, at = (s0, g0) if g0 < 640 else (s1, g0 - 640)
                to[b, z, :, :, :, at : at + size] = part.reshape(4, 4, 16, size)

    def one(which, x, g0, size):
        w = w2[which, g0 : g0 + size, :] if size else wt[which]
        return lax.dot_general(x, w, NT, preferred_element_type=jnp.float32)

    fixed = 8 if slots == 3 else 16

    @pl.loop(0, fixed)
    def _(i):
        apply(i, lambda b, x, tail, g0, size: one(jnp.where(b < 2, core, b - 2), x, g0, size))

    if slots == 3:
        def either(b, x, tail, g0, size):
            flag = tail[:, 624:625].astype(jnp.float32) > 0.5
            return jnp.where(flag, one(1, x, g0, size), one(0, x, g0, size))

        @pl.loop(8, 12)
        def _(i):
            apply(i, either)

    wait_final(2)

    @pl.loop(0, 4 * slots)
    def _(i):
        b, z = i >> 2, i & 3
        full = lax.dot_general(
            f2[b, z].reshape(256, 640), s0[b, z].reshape(256, 640), NT, preferred_element_type=jnp.float32
        )
        tt[b, z] = tt[b, z] + diagonal(full)

    wait_final(3)

    @pl.loop(0, 4 * slots)
    def _(i):
        b, z = i >> 2, i & 3
        full = lax.dot_general(
            f3[b, z].reshape(256, 512),
            s1[b, z, :, :, :, :512].reshape(256, 512),
            NT,
            preferred_element_type=jnp.float32,
        )
        got = diagonal(full) + tt[b, z]
        turned = jnp.where(group == line, got, 0.0)
        for k in range(1, 16):
            shifted = pltpu.roll(pltpu.roll(got, 16 - k, 0), 16 * k, 1)
            turned = jnp.where(group == ((line + k) & 15), shifted, turned)
        for slot in range(16):
            zbuf[b, z, slot >> 2, slot & 3, 0:1] = turned[slot : slot + 1, :128]
            zbuf[b, z, slot >> 2, slot & 3, 1:2] = turned[slot : slot + 1, 128:]
        back_core = jnp.where(b < 2, b, core)
        mine = (z == here[Z]) & (back_core == core)
        src = zbuf.at[b, z]
        dst = ybuf.at[jnp.where(b < 2, core, b), here[Z]]

        @pl.when(mine)
        def _():
            pltpu.make_async_copy(src, dst, back_recv.at[0]).start()

        @pl.when(jnp.logical_not(mine))
        def _():
            pltpu.make_async_remote_copy(
                src, dst, back_send.at[0], back_recv.at[0],
                device_id=dev(moved(Z, z), back_core), device_id_type=MESH,
            ).start()

    pltpu.make_async_copy(ybuf, ybuf, back_recv.at[0]).wait()

    def back(j, k, d):
        axis = ((Y, X) if j < 2 else (X, Y))[k]
        src, dst = ((ybuf, xbuf), (xbuf, dbuf))[k]
        there = (here[axis] + d) & 3
        return pltpu.make_async_remote_copy(
            at_axis(src, j, axis, there), at_axis(dst, j, axis, here[axis]),
            back_send.at[1 + 16 * k + 4 * j + d], back_recv.at[1 + 16 * k + 4 * j + d],
            device_id=dev(moved(axis, there), core), device_id_type=MESH,
        )

    def back_keep(j, k):
        axis = ((Y, X) if j < 2 else (X, Y))[k]
        src, dst = ((ybuf, xbuf), (xbuf, dbuf))[k]
        return pltpu.make_async_copy(
            at_axis(src, j, axis, here[axis]), at_axis(dst, j, axis, here[axis]), back_recv.at[1 + 16 * k + 4 * j]
        )

    for k in range(2):
        for d in (2, 1, 3):
            for j in range(slots):
                back(j, k, d).start()
        for j in range(slots):
            back_keep(j, k).start()
        for j in range(slots):
            back_keep(j, k).wait()
            for d in (1, 3, 2):
                back(j, k, d).wait()

    @pl.loop(0, 4 * slots - (slots - 1))
    def _(_):
        pltpu.make_async_copy(zbuf.at[0, 0], zbuf.at[0, 0], back_send.at[0]).wait()

    out_ref[...] = dbuf[...]


def direct_terms(slots, onehot, flags, row_vc, col_vc, coulomb, val_t, cond_t, screened):
    hbm = pl.BlockSpec(memory_space=pl.ANY)
    vmem = pl.BlockSpec(memory_space=pltpu.VMEM)
    bf16 = jnp.bfloat16
    wide = [(slots, 4, 4, 4, 16, w) for w in WIDTHS]
    small = (slots, 4, 4, 4, 2, 128)
    f32 = jnp.float32
    dma = pltpu.SemaphoreType.DMA
    out = pl.pallas_call(
        functools.partial(place_kernel, slots),
        out_shape=(
            jax.ShapeDtypeStruct(small, f32),
            jax.ShapeDtypeStruct((256, 128), f32),
            *(jax.ShapeDtypeStruct(w, bf16) for w in wide),
            *(jax.ShapeDtypeStruct(w, bf16) for w in wide),
        ),
        in_specs=[vmem, vmem, hbm, vmem, vmem, hbm, hbm, hbm],
        out_specs=(vmem, vmem) + (hbm,) * 8,
        scratch_shapes=[
            pltpu.VMEM(val_t.shape, bf16),
            pltpu.VMEM((16, 48, 128), bf16),
            *(pltpu.VMEM(w, bf16) for w in wide),
            *(pltpu.VMEM(w, bf16) for w in wide),
            pltpu.VMEM((2, 1200, 1200), bf16),
            pltpu.VMEM((2, TILE, 1200), bf16),
            pltpu.VMEM((slots * 64 * 16, TILE), f32),
            pltpu.VMEM((8, 2, 16, 1200), bf16),
            pltpu.VMEM((slots, 4, 16, 256), f32),
            *(pltpu.VMEM(small, f32) for _ in range(4)),
            dma((4,)),
            dma((2,)),
            dma((2, 8)),
            dma((4, 6, 3, 4)),
            dma((4, 6, 2, 4)),
            dma((4, 6, 4)),
            dma((4, 6, 3)),
            dma((33,)),
            dma((33,)),
        ],
        compiler_params=pltpu.CompilerParams(
            collective_id=slots, has_side_effects=True, vmem_limit_bytes=61 * 2**20
        ),
    )(onehot, flags, row_vc, col_vc, coulomb, val_t, cond_t, screened)
    return out[0].reshape(slots * 64, 256), out[1]


def shards(q_index, cond_pairs, val_pairs, row_vc, col_vc, coulomb, screened):
    count = cond_pairs.shape[0]
    slots = 4
    target = q_index[:, 0]
    same = target[:, None] == target[None, :]
    earlier = jnp.arange(count)[None, :] < jnp.arange(count)[:, None]
    rank = jnp.sum((same & earlier).astype(jnp.int32), axis=1)
    core, x, z, y = target & 1, (target >> 1) & 3, (target >> 3) & 3, (target >> 5) & 3
    chip = (z * 4 + y) * 4 + x
    place = (rank * 2 + core) * 64 + chip
    spots = jnp.arange(slots * 64, dtype=jnp.int32)
    onehot = (place[None, :] == spots[:, None]).astype(jnp.bfloat16)
    flags = jnp.broadcast_to(core.astype(jnp.bfloat16)[None, :], (16, count))
    direct, exchange = direct_terms(
        slots, onehot, flags, row_vc, col_vc, coulomb[None, :],
        val_pairs.transpose(1, 2, 0), cond_pairs.transpose(1, 2, 0), screened,
    )
    direct = direct[place].reshape(count, 4, 4, 4, 4).transpose(0, 3, 1, 4, 2).reshape(count, 256)
    exchange = exchange.reshape(16, 16, 8, 16).transpose(0, 2, 1, 3).reshape(count, 256)
    return 2.0 * exchange - direct


def solution(mesh):
    return jax.shard_map(
        shards,
        mesh=mesh,
        in_specs=(
            P(("kb", "col"), None),
            P(("kb", "col"), None, None),
            P(("kb", "col"), None, None),
            P(("kb", "col"), None, None),
            P("col", None, None),
            P(),
            P(("kb", "col"), None, None),
        ),
        out_specs=P(("kb", "col"), None),
        check_vma=False,
    )
```

```python
import functools

import jax
import jax.numpy as jnp
from jax import lax
from jax.experimental import pallas as pl
from jax.experimental.pallas import tpu as pltpu
from jax.sharding import PartitionSpec as P

MESH = pl.DeviceIdType.MESH
Z, Y, X = 0, 1, 2
ORDERS = ((X, Y, Z), (Y, Z, X), (Z, X, Y))
MAIN = 1152
TILE = 128
WIDTHS = (640, 640, 640, 512)
CUTS = ((0, 256, 512, 640), (0, 128, 384, 640), (0, 256, 384, 640), (0, 128, 256, 512))
NT = (((1,), (1,)), ((), ()))


def streams(slots, r):
    out = [(j, ORDERS[j], 0, WIDTHS[r]) for j in range(3)]
    if slots == 4:
        out += [(3, ORDERS[i], CUTS[r][i], CUTS[r][i + 1]) for i in range(3)]
    return out


def at_axis(ref, lead, axis, index, c0=None, c1=None):
    where = [slice(None)] * 3
    where[axis] = index
    return ref.at[(lead, *where, slice(None), slice(c0, c1))]


def fill_slots(buf, st, onehot, slots, tile, chunk_of):
    per = 64 * 16
    for row in range(16):
        st[pl.ds(row, 64 * slots, stride=16), :] = lax.dot_general(
            onehot[: 64 * slots, :], chunk_of(row), NT, preferred_element_type=jnp.float32
        )
    for j in range(slots):
        buf[j, :, :, :, :, pl.ds(pl.multiple_of(tile * TILE, TILE), TILE)] = (
            st[j * per : (j + 1) * per].astype(jnp.bfloat16).reshape(4, 4, 4, 16, TILE)
        )


def prepare_kernel(
    q_ref, val_hbm, cond_hbm, rows_hbm,
    onehot, flag_ref, place_ref, crowd_ref, h10, extra_hbm, s1_hbm, rows_out,
    vt, ct, s0, s1, st, votes, sums, in_sem, row_sem, one_sem, two_sem, send, recv,
):
    kb = lax.axis_index("kb")
    col = lax.axis_index("col")
    here = (kb & 3, kb >> 2, col >> 1)
    load_val = pltpu.make_async_copy(val_hbm, vt, in_sem.at[0])
    load_val.start()
    load_tail = pltpu.make_async_copy(cond_hbm.at[:, MAIN:], ct, in_sem.at[2])
    load_tail.start()
    own_rows = pltpu.make_async_copy(rows_hbm, rows_out.at[col], in_sem.at[1])
    own_rows.start()

    def mate(d):
        return (kb, (col + d) & 7)

    def far(d):
        return ((kb + d) & 15, col)

    barrier = pltpu.get_barrier_semaphore()
    for d in range(1, 8):
        pl.semaphore_signal(barrier, inc=1, device_id=mate(d), device_id_type=MESH)
    for d in range(1, 16):
        pl.semaphore_signal(barrier, inc=1, device_id=far(d), device_id_type=MESH)

    size = q_ref.shape[1]
    along = jnp.broadcast_to(q_ref[...], (size, size))
    before = lax.broadcasted_iota(jnp.int32, (size, size), 0) < lax.broadcasted_iota(jnp.int32, (size, size), 1)

    def turned(a):
        return jnp.transpose(a.astype(jnp.float32)).astype(jnp.int32)

    down = turned(along)
    repeat = jnp.sum(jnp.where((along == down) & before, 1.0, 0.0), axis=0, keepdims=True)
    repeats = jnp.broadcast_to(repeat, (size, size)).astype(jnp.int32)
    both = ((along >> 1) == (down >> 1)) & before & (repeats > 0) & (turned(repeats) > 0)
    more = jnp.sum(jnp.where(both, 1.0, 0.0), axis=0, keepdims=True)
    q = q_ref[...]
    core, x, z, y = q & 1, (q >> 1) & 3, (q >> 3) & 3, (q >> 5) & 3
    chip = (z * 4 + y) * 4 + x
    slot = jnp.where(repeat > 0.5, 2 + more.astype(jnp.int32), core)
    place = slot * 64 + chip
    place_ref[...] = slot + ((((y * 4 + x) * 4) + z) << 2)
    flag_ref[...] = jnp.broadcast_to(core.astype(jnp.float32), (16, size)).astype(jnp.bfloat16)
    spots = lax.broadcasted_iota(jnp.int32, onehot.shape, 0)
    onehot[...] = jnp.where(spots == place, 1.0, 0.0).astype(jnp.bfloat16)
    votes[0] = jnp.broadcast_to(jnp.max(more, axis=1, keepdims=True), (8, TILE))

    pl.semaphore_wait(barrier, 22)

    def first(d):
        return pltpu.make_async_remote_copy(
            votes.at[0], votes.at[d], one_sem.at[0, d], one_sem.at[1, d], device_id=mate(d), device_id_type=MESH
        )

    def second(d):
        return pltpu.make_async_remote_copy(
            sums.at[0], sums.at[d], two_sem.at[0, d], two_sem.at[1, d], device_id=far(d), device_id_type=MESH
        )

    def row_copy(d):
        return pltpu.make_async_remote_copy(
            rows_hbm, rows_out.at[col], row_sem.at[0, d], row_sem.at[1, d], device_id=mate(d), device_id_type=MESH
        )

    for d in range(1, 8):
        first(d).start()
    for d in range(1, 8):
        row_copy(d).start()

    load_val.wait()

    def ring(part, j, d):
        c0, c1 = ((0, 256), (256, 640))[part]
        axis = ORDERS[j][0]
        chip = list(here)
        chip[axis] = (here[axis] + d) & 3
        return pltpu.make_async_remote_copy(
            at_axis(s0, j, axis, chip[axis], c0, c1), at_axis(h10, j, axis, here[axis], c0, c1),
            send.at[part, j, d], recv.at[part, j, d],
            device_id=(chip[Y] * 4 + chip[Z], chip[X] * 2 + (col & 1)), device_id_type=MESH,
        )

    def keep(j):
        axis = ORDERS[j][0]
        return pltpu.make_async_copy(
            at_axis(s0, j, axis, here[axis]), at_axis(h10, j, axis, here[axis]), recv.at[0, j, 0]
        )

    for part, (lo, hi) in enumerate(((0, 2), (2, 5))):
        @pl.loop(lo, hi)
        def _(t):
            fill_slots(s0, st, onehot, 4, t, lambda row: vt[row, pl.ds(pl.multiple_of(t * TILE, TILE), TILE), :])

        if part == 1:
            for d in range(1, 8):
                first(d).wait()
            sums[0] = jnp.max(votes[...], axis=0)
            for d in range(1, 16):
                second(d).start()
        for d in (1, 3, 2):
            for j in range(3):
                ring(part, j, d).start()
    for j in range(3):
        keep(j).start()
    store_extra = pltpu.make_async_copy(s0.at[3], extra_hbm.at[0], in_sem.at[3])
    store_extra.start()

    @pl.loop(0, 4)
    def _(t):
        fill_slots(
            s1, st, onehot, 4, t, lambda row: vt[row, pl.ds(pl.multiple_of(640 + t * TILE, TILE), TILE), :]
        )

    load_tail.wait()
    gap = jnp.zeros((16, TILE), jnp.bfloat16)
    fill_slots(
        s1, st, onehot, 4, 4,
        lambda row: jnp.concatenate([vt[row, MAIN:, :], gap, ct[row], flag_ref[...]], axis=0),
    )
    store = pltpu.make_async_copy(s1, s1_hbm, in_sem.at[4])
    store.start()
    for d in range(1, 16):
        second(d).wait()
    crowd_ref[...] = jnp.max(sums[...], axis=0)
    own_rows.wait()
    for d in range(1, 8):
        row_copy(d).wait()
    store_extra.wait()
    store.wait()
    for j in range(3):
        for d in (1, 3, 2):
            for part in range(2):
                ring(part, j, d).wait()
        keep(j).wait()


def prepare(q_row, val_t, cond_t, row_vc):
    hbm = pl.BlockSpec(memory_space=pl.ANY)
    vmem = pl.BlockSpec(memory_space=pltpu.VMEM)
    bf16, f32 = jnp.bfloat16, jnp.float32
    count = q_row.shape[1]
    first = (4, 4, 4, 4, 16, WIDTHS[0])
    dma = pltpu.SemaphoreType.DMA
    return pl.pallas_call(
        prepare_kernel,
        out_shape=(
            jax.ShapeDtypeStruct((256, count), bf16),
            jax.ShapeDtypeStruct((16, count), bf16),
            jax.ShapeDtypeStruct((1, count), jnp.int32),
            jax.ShapeDtypeStruct((8, TILE), f32),
            jax.ShapeDtypeStruct((3,) + first[1:], bf16),
            jax.ShapeDtypeStruct((1,) + first[1:], bf16),
            jax.ShapeDtypeStruct(first, bf16),
            jax.ShapeDtypeStruct((8,) + row_vc.shape, bf16),
        ),
        in_specs=[vmem, hbm, hbm, hbm],
        out_specs=(vmem, vmem, vmem, vmem, hbm, hbm, hbm, hbm),
        scratch_shapes=[
            pltpu.VMEM(val_t.shape, bf16),
            pltpu.VMEM((16, val_t.shape[1] - MAIN, count), bf16),
            pltpu.VMEM(first, bf16),
            pltpu.VMEM(first, bf16),
            pltpu.VMEM((256 * 16, TILE), f32),
            pltpu.VMEM((8, 8, TILE), f32),
            pltpu.VMEM((16, 8, TILE), f32),
            dma((5,)),
            dma((2, 8)),
            dma((2, 8)),
            dma((2, 16)),
            dma((2, 3, 4)),
            dma((2, 3, 4)),
        ],
        compiler_params=pltpu.CompilerParams(
            collective_id=1, has_side_effects=True, vmem_limit_bytes=48 * 2**20
        ),
    )(q_row, val_t, cond_t, row_vc)


def place_kernel(
    slots,
    onehot, rows_hbm, cols_ref, coulomb_ref, h10, extra_hbm, s1_hbm, cond_hbm, w_hbm,
    out_ref, ex_ref, h10x, h11, h12, h13, h20, h21, h22, h23,
    vt, bounce, s0, s1, s2, s3, f0, f1, f2, f3, w2, wt, st, rows, tt, zbuf, ybuf, dbuf,
    in_sem, w_sem, send, recv, last, local, local_on, back_send, back_recv,
):
    kb = lax.axis_index("kb")
    col = lax.axis_index("col")
    here = (kb & 3, kb >> 2, col >> 1)
    core = col & 1

    def dev(chip, which):
        return (chip[Y] * 4 + chip[Z], chip[X] * 2 + which)

    def moved(axis, index):
        chip = list(here)
        chip[axis] = index
        return tuple(chip)

    load_cond = pltpu.make_async_copy(cond_hbm.at[:, :MAIN], vt, in_sem.at[0])
    load_cond.start()
    load_w = pltpu.make_async_copy(w_hbm.at[0], w2.at[core], in_sem.at[2])
    load_w.start()
    load_rows = pltpu.make_async_copy(rows_hbm, rows, in_sem.at[3])
    load_rows.start()

    barrier = pltpu.get_barrier_semaphore()
    for axis in range(3):
        for d in (1, 2, 3):
            for which in range(2):
                pl.semaphore_signal(
                    barrier, inc=1, device_id=dev(moved(axis, (here[axis] + d) & 3), which), device_id_type=MESH
                )
    pl.semaphore_signal(barrier, inc=1, device_id=dev(here, 1 - core), device_id_type=MESH)

    def across(dy, dx):
        return (here[Z], (here[Y] + dy) & 3, (here[X] + dx) & 3)

    for dy in (1, 2, 3):
        for dx in (1, 2, 3):
            pl.semaphore_signal(barrier, inc=1, device_id=dev(across(dy, dx), core), device_id_type=MESH)

    rounds = ((extra_hbm, h10x, h20, f0), (s1_hbm, h11, h21, f1), (s2, h12, h22, f2), (s3, h13, h23, f3))
    parts = tuple(streams(slots, r) for r in range(4))
    n_streams = len(parts[0])

    def build(buf, first, tiles):
        @pl.loop(0, tiles)
        def _(t):
            fill_slots(buf, st, onehot, slots, t, lambda row: vt[row, pl.ds(pl.multiple_of((first + t) * TILE, TILE), TILE), :])

    def held(r, j, k):
        if r == 0 and k < 2:
            return (h10, j) if j < 3 else (rounds[0][k], 0)
        return rounds[r][k], j

    def ring(r, s, k, d):
        j, order, c0, c1 = parts[r][s]
        axis = order[k]
        there = (here[axis] + d) & 3
        return pltpu.make_async_remote_copy(
            at_axis(*held(r, j, k), axis, there, c0, c1),
            at_axis(*held(r, j, k + 1), axis, here[axis], c0, c1),
            send.at[r, s, k, d], recv.at[r, s, k, d],
            device_id=dev(moved(axis, there), core), device_id_type=MESH,
        )

    def keep(r, s, k):
        j, order, c0, c1 = parts[r][s]
        axis = order[k]
        src = at_axis(*held(r, j, k), axis, here[axis], c0, c1)
        dst = at_axis(*held(r, j, k + 1), axis, here[axis], c0, c1)
        if k == 0 and r > 1:
            return (pltpu.make_async_copy(src, dst, local.at[r, s, k]),)
        via = bounce.at[r % 2, j, :, :, :, c0:c1]
        return (
            pltpu.make_async_copy(src, via, local.at[r, s, k]),
            pltpu.make_async_copy(via, dst, local_on.at[r, s, k]),
        )

    def start_ring(r, k, lo=0, hi=n_streams):
        for d in (1, 3, 2):
            for s in range(lo, hi):
                ring(r, s, k, d).start()
        for s in range(lo, hi):
            keep(r, s, k)[0].start()

    def wait_ring(r, k, lo=0, hi=n_streams):
        for s in range(lo, hi):
            own = keep(r, s, k)
            own[0].wait()
            if len(own) > 1:
                own[1].start()
        for s in range(lo, hi):
            for d in (1, 3, 2):
                c = ring(r, s, k, d)
                c.wait_send()
                c.wait_recv()
            own = keep(r, s, k)
            if len(own) > 1:
                own[1].wait()

    def final(r, s, d):
        j, order, c0, c1 = parts[r][s]
        axis = order[2]
        there = (here[axis] + d) & 3
        lead, goal = (core, j) if j < 2 else (j, core)
        sem = last.at[r, lead, d] if j < 2 else last.at[r, s, d]
        return pltpu.make_async_remote_copy(
            at_axis(rounds[r][2], j, axis, there, c0, c1),
            at_axis(rounds[r][3], lead, axis, here[axis], c0, c1),
            send.at[r, s, 2, d], sem,
            device_id=dev(moved(axis, there), goal), device_id_type=MESH,
        )

    def final_local(r, s):
        j, order, c0, c1 = parts[r][s]
        axis = order[2]
        lead = core if j < 2 else j
        return pltpu.make_async_copy(
            at_axis(rounds[r][2], j, axis, here[axis], c0, c1),
            at_axis(rounds[r][3], lead, axis, here[axis], c0, c1),
            local.at[r, s, 2],
        )

    def start_final(r):
        for d in (1, 3, 2):
            for s in range(n_streams):
                final(r, s, d).start()
        for s in range(n_streams):
            if s < 2:
                @pl.when(core == s)
                def _():
                    final_local(r, s).start()

                @pl.when(core != s)
                def _():
                    final(r, s, 0).start()
            else:
                final_local(r, s).start()

    def wait_final(r):
        for s in range(n_streams):
            for d in (1, 3, 2):
                final(r, s, d).wait_send()
            if s < 2:
                @pl.when(core == s)
                def _():
                    final_local(r, s).wait()

                @pl.when(core != s)
                def _():
                    final(r, s, 0).wait_send()
            else:
                final_local(r, s).wait()
                for d in (1, 3, 2):
                    final(r, s, d).wait_recv()
        for mine in range(2):
            axis = ORDERS[mine][2]

            @pl.when(core == mine)
            def _():
                for lead in range(2):
                    for d in (1, 3, 2) if lead == mine else (1, 3, 2, 0):
                        at = at_axis(rounds[r][3], lead, axis, here[axis])
                        pltpu.make_async_remote_copy(
                            at, at, send.at[r, mine, 2, d], last.at[r, lead, d],
                            device_id=dev(here, 1 - core), device_id_type=MESH,
                        ).wait_recv()

    pl.semaphore_wait(barrier, 28)
    start_ring(0, 1, 0, 3)
    start_ring(0, 0, 3)
    start_ring(1, 0)
    send_w = pltpu.make_async_remote_copy(
        w_hbm.at[0], w2.at[core], w_sem.at[0], w_sem.at[1], device_id=dev(here, 1 - core), device_id_type=MESH
    )
    send_w.start()
    load_cond.wait()
    build(s2, 0, 5)
    wait_ring(0, 0, 3)
    start_ring(0, 1, 3)
    start_ring(2, 0)
    build(s3, 5, 4)
    wait_ring(1, 0)
    start_ring(1, 1)
    start_ring(3, 0)

    load_rows.wait()
    scaled = (cols_ref[...].astype(jnp.float32) * coulomb_ref[...][None]).astype(jnp.bfloat16)
    ex_ref[...] = lax.dot_general(
        rows[...].reshape(256, 1200), scaled.reshape(128, 1200), NT, preferred_element_type=jnp.float32
    )
    load_w.wait()
    send_w.wait()
    wt[...] = jnp.zeros_like(wt)
    for which in range(2):
        wt[which, 64:112] = w2[which, MAIN:]

    wait_ring(0, 1)
    start_final(0)
    wait_ring(2, 0)
    start_ring(2, 1)
    wait_ring(1, 1)
    start_final(1)
    wait_ring(3, 0)
    start_ring(3, 1)
    wait_ring(2, 1)
    start_final(2)
    wait_final(0)
    wait_ring(3, 1)
    start_final(3)
    wait_final(1)

    group = lax.broadcasted_iota(jnp.int32, (16, 256), 1) >> 4
    line = lax.broadcasted_iota(jnp.int32, (16, 256), 0)

    def diagonal(full):
        total = jnp.zeros((16, 256), jnp.float32)
        for i in range(16):
            total = jnp.where(group == i, full[16 * i : 16 * i + 16], total)
        return total

    def apply(i, times):
        b, z = i >> 2, i & 3
        tail = f1[b, z].reshape(256, 640)
        x = jnp.concatenate([f0[b, z].reshape(256, 640), tail], axis=1)[:, :1200]
        for n, (g0, size) in enumerate(((0, 256), (256, 256), (512, 128), (640, 256), (896, 256), (0, 0))):
            part = times(b, x, tail, g0, size).astype(jnp.bfloat16)
            if size == 0:
                s1[b, z, :, :, :, 512:640] = part.reshape(4, 4, 16, 128)
                tt[b, z] = diagonal(lax.dot_general(tail[:, 512:], part, NT, preferred_element_type=jnp.float32))
            else:
                to, at = (s0, g0) if g0 < 640 else (s1, g0 - 640)
                to[b, z, :, :, :, at : at + size] = part.reshape(4, 4, 16, size)

    def one(which, x, g0, size):
        w = w2[which, g0 : g0 + size, :] if size else wt[which]
        return lax.dot_general(x, w, NT, preferred_element_type=jnp.float32)

    @pl.loop(0, 8)
    def _(i):
        apply(i, lambda b, x, tail, g0, size: one(core, x, g0, size))

    def either(b, x, tail, g0, size):
        flag = tail[:, 624:625].astype(jnp.float32) > 0.5
        return jnp.where(flag, one(1, x, g0, size), one(0, x, g0, size))

    @pl.loop(8, 4 * slots)
    def _(i):
        apply(i, either)

    wait_final(2)

    @pl.loop(0, 4 * slots)
    def _(i):
        b, z = i >> 2, i & 3
        full = lax.dot_general(
            f2[b, z].reshape(256, 640), s0[b, z].reshape(256, 640), NT, preferred_element_type=jnp.float32
        )
        tt[b, z] = tt[b, z] + diagonal(full)

    wait_final(3)

    @pl.loop(0, 4 * slots)
    def _(i):
        b, z = i >> 2, i & 3
        full = lax.dot_general(
            f3[b, z].reshape(256, 512),
            s1[b, z, :, :, :, :512].reshape(256, 512),
            NT,
            preferred_element_type=jnp.float32,
        )
        got = diagonal(full) + tt[b, z]
        turned = jnp.where(group == line, got, 0.0)
        for k in range(1, 16):
            shifted = pltpu.roll(pltpu.roll(got, 16 - k, 0), 16 * k, 1)
            turned = jnp.where(group == ((line + k) & 15), shifted, turned)
        for slot in range(16):
            zbuf[b, z, slot >> 2, slot & 3, 0:1] = turned[slot : slot + 1, :128]
            zbuf[b, z, slot >> 2, slot & 3, 1:2] = turned[slot : slot + 1, 128:]
        back_core = jnp.where(b < 2, b, core)
        mine = (z == here[Z]) & (back_core == core)
        src = zbuf.at[b, z]
        dst = ybuf.at[:, :, jnp.where(b < 2, core, b), here[Z]]

        @pl.when(mine)
        def _():
            pltpu.make_async_copy(src, dst, back_recv.at[0]).start()

        @pl.when(jnp.logical_not(mine))
        def _():
            pltpu.make_async_remote_copy(
                src, dst, back_send.at[0], back_recv.at[0],
                device_id=dev(moved(Z, z), back_core), device_id_type=MESH,
            ).start()

    pltpu.make_async_copy(ybuf, ybuf, back_recv.at[0]).wait()
    back_own = pltpu.make_async_copy(ybuf.at[here[Y], here[X]], dbuf.at[here[Y], here[X]], back_recv.at[16])
    back_own.start()

    def back(dy, dx):
        chip = across(dy, dx)
        return pltpu.make_async_remote_copy(
            ybuf.at[chip[Y], chip[X]], dbuf.at[here[Y], here[X]],
            back_send.at[4 * dy + dx], back_recv.at[4 * dy + dx],
            device_id=dev(chip, core), device_id_type=MESH,
        )

    ways = [(dy, dx) for dy in (2, 1, 3, 0) for dx in (2, 1, 3, 0) if dy or dx]
    for way in ways:
        back(*way).start()
    back_own.wait()
    for way in ways:
        back(*way).wait()

    @pl.loop(0, 4 * slots - (slots - 1))
    def _(_):
        pltpu.make_async_copy(zbuf.at[0, 0], zbuf.at[0, 0], back_send.at[0]).wait()

    out_ref[...] = dbuf[...]


def direct_terms(slots, onehot, rows, col_vc, coulomb, h10, extra, second, cond_t, screened):
    hbm = pl.BlockSpec(memory_space=pl.ANY)
    vmem = pl.BlockSpec(memory_space=pltpu.VMEM)
    bf16, f32 = jnp.bfloat16, jnp.float32
    wide = [(slots, 4, 4, 4, 16, w) for w in WIDTHS]
    back = (4, 4, slots, 4, 2, 128)
    dma = pltpu.SemaphoreType.DMA
    out = pl.pallas_call(
        functools.partial(place_kernel, slots),
        out_shape=(
            jax.ShapeDtypeStruct(back, f32),
            jax.ShapeDtypeStruct((256, 128), f32),
            jax.ShapeDtypeStruct(extra.shape, bf16),
            *(jax.ShapeDtypeStruct(w, bf16) for w in wide[1:]),
            *(jax.ShapeDtypeStruct(w, bf16) for w in wide),
        ),
        in_specs=[vmem, hbm, vmem, vmem, hbm, hbm, hbm, hbm, hbm],
        out_specs=(vmem, vmem) + (hbm,) * 8,
        scratch_shapes=[
            pltpu.VMEM((16, MAIN, cond_t.shape[2]), bf16),
            pltpu.VMEM((2, slots, 4, 4, 16, WIDTHS[0]), bf16),
            *(pltpu.VMEM(w, bf16) for w in wide),
            *(pltpu.VMEM(w, bf16) for w in wide),
            pltpu.VMEM((2, 1200, 1200), bf16),
            pltpu.VMEM((2, TILE, 1200), bf16),
            pltpu.VMEM((slots * 64 * 16, TILE), f32),
            pltpu.VMEM(rows.shape, bf16),
            pltpu.VMEM((slots, 4, 16, 256), f32),
            pltpu.VMEM((slots, 4, 4, 4, 2, 128), f32),
            pltpu.VMEM(back, f32),
            pltpu.VMEM(back, f32),
            dma((4,)),
            dma((2,)),
            dma((4, 6, 3, 4)),
            dma((4, 6, 2, 4)),
            dma((4, 6, 4)),
            dma((4, 6, 3)),
            dma((4, 6, 3)),
            dma((17,)),
            dma((17,)),
        ],
        compiler_params=pltpu.CompilerParams(
            collective_id=slots, has_side_effects=True, vmem_limit_bytes=61 * 2**20
        ),
    )(onehot, rows, col_vc, coulomb, h10, extra, second, cond_t, screened)
    return out[0].reshape(slots * 64, 256), out[1]


def shards(q_index, cond_pairs, val_pairs, row_vc, col_vc, coulomb, screened):
    count = cond_pairs.shape[0]
    val_t = val_pairs.transpose(1, 2, 0)
    cond_t = cond_pairs.transpose(1, 2, 0)
    onehot, _, place, crowd, h10, extra, second, rows = prepare(q_index.reshape(1, count), val_t, cond_t, row_vc)
    slot, chip = place[0] & 3, place[0] >> 2

    def move(slots, *args):
        direct, exchange = direct_terms(slots, *args)
        return direct[((chip >> 2) * slots + slot) * 4 + (chip & 3)], exchange

    direct, exchange = lax.cond(
        crowd[0, 0] > 0.5, functools.partial(move, 4), functools.partial(move, 3),
        onehot, rows, col_vc, coulomb[None, :], h10, extra, second, cond_t, screened,
    )
    direct = direct.reshape(count, 4, 4, 4, 4).transpose(0, 3, 1, 4, 2).reshape(count, 256)
    exchange = exchange.reshape(16, 16, 8, 16).transpose(0, 2, 1, 3).reshape(count, 256)
    return 2.0 * exchange - direct


def solution(mesh):
    return jax.shard_map(
        shards,
        mesh=mesh,
        in_specs=(
            P(("kb", "col"), None),
            P(("kb", "col"), None, None),
            P(("kb", "col"), None, None),
            P(("kb", "col"), None, None),
            P("col", None, None),
            P(),
            P(("kb", "col"), None, None),
        ),
        out_specs=P(("kb", "col"), None),
        check_vma=False,
    )
```

```python
import functools

import jax
import jax.numpy as jnp
from jax import lax
from jax.experimental import pallas as pl
from jax.experimental.pallas import tpu as pltpu
from jax.sharding import PartitionSpec as P

MESH = pl.DeviceIdType.MESH
Z, Y, X = 0, 1, 2
ORDERS = ((X, Y, Z), (Y, Z, X), (Z, X, Y))
MAIN = 1152
TILE = 128
WIDTHS = (640, 640, 640, 512)
CUTS = ((0, 256, 512, 640), (0, 128, 384, 640), (0, 256, 384, 640), (0, 128, 256, 512))
NT = (((1,), (1,)), ((), ()))


def streams(slots, r):
    if slots == 3:
        return [(j, ORDERS[j], 0, WIDTHS[r]) for j in range(3)]
    return [(0, ORDERS[i], CUTS[r][i], CUTS[r][i + 1]) for i in range(3)]


def at_axis(ref, lead, axis, index, c0=None, c1=None):
    where = [slice(None)] * 3
    where[axis] = index
    return ref.at[(lead, *where, slice(None), slice(c0, c1))]


def fill_slots(buf, st, onehot, slots, tile, chunk_of):
    per = 64 * 16
    for row in range(16):
        st[pl.ds(row, 64 * slots, stride=16), :] = lax.dot_general(
            onehot[: 64 * slots, :], chunk_of(row), NT, preferred_element_type=jnp.float32
        )
    for j in range(slots):
        buf[j, :, :, :, :, pl.ds(pl.multiple_of(tile * TILE, TILE), TILE)] = (
            st[j * per : (j + 1) * per].astype(jnp.bfloat16).reshape(4, 4, 4, 16, TILE)
        )


def find_places(q_ref, onehot, flag_ref, place_ref, votes):
    size = q_ref.shape[1]
    along = jnp.broadcast_to(q_ref[...], (size, size))
    before = lax.broadcasted_iota(jnp.int32, (size, size), 0) < lax.broadcasted_iota(jnp.int32, (size, size), 1)

    def turned(a):
        return jnp.transpose(a.astype(jnp.float32)).astype(jnp.int32)

    down = turned(along)
    repeat = jnp.sum(jnp.where((along == down) & before, 1.0, 0.0), axis=0, keepdims=True)
    repeats = jnp.broadcast_to(repeat, (size, size)).astype(jnp.int32)
    both = ((along >> 1) == (down >> 1)) & before & (repeats > 0) & (turned(repeats) > 0)
    more = jnp.sum(jnp.where(both, 1.0, 0.0), axis=0, keepdims=True)
    q = q_ref[...]
    core, x, z, y = q & 1, (q >> 1) & 3, (q >> 3) & 3, (q >> 5) & 3
    slot = jnp.where(repeat > 0.5, 2 + more.astype(jnp.int32), core)
    place_ref[...] = slot + ((((y * 4 + x) * 4) + z) << 2)
    flag_ref[...] = jnp.broadcast_to(core.astype(jnp.float32), (16, size)).astype(jnp.bfloat16)
    spots = lax.broadcasted_iota(jnp.int32, onehot.shape, 0)
    onehot[...] = jnp.where(spots == slot * 64 + (z * 4 + y) * 4 + x, 1.0, 0.0).astype(jnp.bfloat16)
    votes[0] = jnp.broadcast_to(jnp.max(more, axis=1, keepdims=True), (8, TILE))


def place_kernel(slots, *refs):
    whole = slots == 3
    if whole:
        (q_ref, rows_hbm, cols_ref, coulomb_ref, val_hbm, cond_hbm, w_hbm,
         out_ref, ex_ref, onehot, flag_ref, place_ref, crowd_ref), refs = refs[:13], refs[13:]
    else:
        (onehot, flag_ref, val_hbm, cond_hbm, w_hbm, out_ref), refs = refs[:6], refs[6:]
    (h10, h11, h12, h13, h20, h21, h22, h23,
     vt, ct, bounce, s0, s1, s2, s3, f0, f1, f2, f3, w2, wt, st, tt, zbuf, ybuf, dbuf,
     in_sem, w_sem, send, recv, last, local, local_on, back_send, back_recv), refs = refs[:35], refs[35:]
    if whole:
        rows, votes, sums, row_sem, one_sem, two_sem = refs
    kb = lax.axis_index("kb")
    col = lax.axis_index("col")
    here = (kb & 3, kb >> 2, col >> 1)
    core = col & 1

    def dev(chip, which):
        return (chip[Y] * 4 + chip[Z], chip[X] * 2 + which)

    def moved(axis, index):
        chip = list(here)
        chip[axis] = index
        return tuple(chip)

    load_val = pltpu.make_async_copy(val_hbm, vt, in_sem.at[0])
    load_val.start()
    load_tail = pltpu.make_async_copy(cond_hbm.at[:, MAIN:], ct, in_sem.at[1])
    load_tail.start()
    load_w = pltpu.make_async_copy(w_hbm.at[0], w2.at[core], in_sem.at[2])
    load_w.start()

    barrier = pltpu.get_barrier_semaphore()
    for axis in range(3):
        for d in (1, 2, 3):
            for which in range(2):
                pl.semaphore_signal(
                    barrier, inc=1, device_id=dev(moved(axis, (here[axis] + d) & 3), which), device_id_type=MESH
                )
    pl.semaphore_signal(barrier, inc=1, device_id=dev(here, 1 - core), device_id_type=MESH)

    def across(dy, dx):
        return (here[Z], (here[Y] + dy) & 3, (here[X] + dx) & 3)

    for dy in (1, 2, 3):
        for dx in (1, 2, 3):
            pl.semaphore_signal(barrier, inc=1, device_id=dev(across(dy, dx), core), device_id_type=MESH)

    def mate(d):
        return (kb, (col + d) & 7)

    def far(d):
        return (((kb >> 2) + (d >> 2) & 3) * 4 + ((kb + d) & 3), col)

    if whole:
        for d in range(5, 16):
            if d & 3:
                pl.semaphore_signal(barrier, inc=1, device_id=far(d), device_id_type=MESH)
        load_rows = pltpu.make_async_copy(rows_hbm, rows.at[col], in_sem.at[3])
        load_rows.start()
        find_places(q_ref, onehot, flag_ref, place_ref, votes)

    rounds = ((s0, h10, h20, f0), (s1, h11, h21, f1), (s2, h12, h22, f2), (s3, h13, h23, f3))
    parts = tuple(streams(slots, r) for r in range(4))
    n_streams = 3

    def build(buf, first, tiles):
        @pl.loop(0, tiles)
        def _(t):
            fill_slots(buf, st, onehot, slots, t, lambda row: vt[row, pl.ds(pl.multiple_of((first + t) * TILE, TILE), TILE), :])

    def held(r, j, k):
        return rounds[r][k], j

    def ring(r, s, k, d):
        j, order, c0, c1 = parts[r][s]
        axis = order[k]
        there = (here[axis] + d) & 3
        return pltpu.make_async_remote_copy(
            at_axis(*held(r, j, k), axis, there, c0, c1),
            at_axis(*held(r, j, k + 1), axis, here[axis], c0, c1),
            send.at[r, s, k, d], recv.at[r, s, k, d],
            device_id=dev(moved(axis, there), core), device_id_type=MESH,
        )

    def keep(r, s, k):
        j, order, c0, c1 = parts[r][s]
        axis = order[k]
        src = at_axis(*held(r, j, k), axis, here[axis], c0, c1)
        dst = at_axis(*held(r, j, k + 1), axis, here[axis], c0, c1)
        if k == 0:
            return (pltpu.make_async_copy(src, dst, local.at[r, s, k]),)
        via = bounce.at[r % 2, j, :, :, :, c0:c1]
        return (
            pltpu.make_async_copy(src, via, local.at[r, s, k]),
            pltpu.make_async_copy(via, dst, local_on.at[r, s, k]),
        )

    def start_ring(r, k, lo=0, hi=n_streams):
        for d in (1, 3, 2):
            for s in range(lo, hi):
                ring(r, s, k, d).start()
        for s in range(lo, hi):
            keep(r, s, k)[0].start()

    def wait_ring(r, k, lo=0, hi=n_streams):
        for s in range(lo, hi):
            own = keep(r, s, k)
            own[0].wait()
            if len(own) > 1:
                own[1].start()
        for s in range(lo, hi):
            for d in (1, 3, 2):
                c = ring(r, s, k, d)
                c.wait_send()
                c.wait_recv()
            own = keep(r, s, k)
            if len(own) > 1:
                own[1].wait()

    def final(r, s, d):
        j, order, c0, c1 = parts[r][s]
        axis = order[2]
        there = (here[axis] + d) & 3
        lead, goal = (core, j) if whole and j < 2 else (j, core)
        sem = last.at[r, lead, d] if whole and j < 2 else last.at[r, s, d]
        return pltpu.make_async_remote_copy(
            at_axis(rounds[r][2], j, axis, there, c0, c1),
            at_axis(rounds[r][3], lead, axis, here[axis], c0, c1),
            send.at[r, s, 2, d], sem,
            device_id=dev(moved(axis, there), goal), device_id_type=MESH,
        )

    def final_local(r, s):
        j, order, c0, c1 = parts[r][s]
        axis = order[2]
        lead = core if whole and j < 2 else j
        return pltpu.make_async_copy(
            at_axis(rounds[r][2], j, axis, here[axis], c0, c1),
            at_axis(rounds[r][3], lead, axis, here[axis], c0, c1),
            local.at[r, s, 2],
        )

    def start_final(r):
        for d in (1, 3, 2):
            for s in range(n_streams):
                final(r, s, d).start()
        for s in range(n_streams):
            if whole and s < 2:
                @pl.when(core == s)
                def _():
                    final_local(r, s).start()

                @pl.when(core != s)
                def _():
                    final(r, s, 0).start()
            else:
                final_local(r, s).start()

    def wait_final(r):
        for s in range(n_streams):
            for d in (1, 3, 2):
                final(r, s, d).wait_send()
            if whole and s < 2:
                @pl.when(core == s)
                def _():
                    final_local(r, s).wait()

                @pl.when(core != s)
                def _():
                    final(r, s, 0).wait_send()
            else:
                final_local(r, s).wait()
                for d in (1, 3, 2):
                    final(r, s, d).wait_recv()
        for mine in range(2 if whole else 0):
            axis = ORDERS[mine][2]

            @pl.when(core == mine)
            def _():
                for lead in range(2):
                    for d in (1, 3, 2) if lead == mine else (1, 3, 2, 0):
                        at = at_axis(rounds[r][3], lead, axis, here[axis])
                        pltpu.make_async_remote_copy(
                            at, at, send.at[r, mine, 2, d], last.at[r, lead, d],
                            device_id=dev(here, 1 - core), device_id_type=MESH,
                        ).wait_recv()

    def vote(d):
        return pltpu.make_async_remote_copy(
            votes.at[0], votes.at[d], one_sem.at[0, d], one_sem.at[1, d], device_id=mate(d), device_id_type=MESH
        )

    def count_votes(d):
        return pltpu.make_async_remote_copy(
            sums.at[0], sums.at[d], two_sem.at[0, d], two_sem.at[1, d], device_id=far(d), device_id_type=MESH
        )

    def row_copy(d):
        return pltpu.make_async_remote_copy(
            rows_hbm, rows.at[col], row_sem.at[0, d], row_sem.at[1, d], device_id=mate(d), device_id_type=MESH
        )

    pl.semaphore_wait(barrier, 37 if whole else 28)
    if whole:
        for d in range(1, 8):
            vote(d).start()
        for d in range(1, 8):
            row_copy(d).start()
    load_val.wait()
    build(s0, 0, 5)
    start_ring(0, 0)
    load_tail.wait()
    build(s1, 5, 4)
    gap = jnp.zeros((16, TILE), jnp.bfloat16)
    fill_slots(
        s1, st, onehot, slots, 4,
        lambda row: jnp.concatenate([vt[row, MAIN:, :], gap, ct[row], flag_ref[...]], axis=0),
    )
    load_cond = pltpu.make_async_copy(cond_hbm, vt, in_sem.at[0])
    load_cond.start()
    start_ring(1, 0)
    send_w = pltpu.make_async_remote_copy(
        w_hbm.at[0], w2.at[core], w_sem.at[0], w_sem.at[1], device_id=dev(here, 1 - core), device_id_type=MESH
    )
    send_w.start()
    if whole:
        for d in range(1, 8):
            vote(d).wait()
        sums[0] = jnp.max(votes[...], axis=0)
        for d in range(1, 16):
            count_votes(d).start()
    load_cond.wait()
    build(s2, 0, 5)
    wait_ring(0, 0)
    start_ring(0, 1)
    start_ring(2, 0)
    build(s3, 5, 4)
    wait_ring(1, 0)
    start_ring(1, 1)
    start_ring(3, 0)

    if whole:
        load_rows.wait()
        for d in range(1, 8):
            row_copy(d).wait()
        scaled = (cols_ref[...].astype(jnp.float32) * coulomb_ref[...][None]).astype(jnp.bfloat16)
        ex_ref[...] = lax.dot_general(
            rows[...].reshape(256, 1200), scaled.reshape(128, 1200), NT, preferred_element_type=jnp.float32
        )
        for d in range(1, 16):
            count_votes(d).wait()
        crowd_ref[...] = jnp.max(sums[...], axis=0)
    load_w.wait()
    send_w.wait()
    wt[...] = jnp.zeros_like(wt)
    for which in range(2):
        wt[which, 64:112] = w2[which, MAIN:]

    wait_ring(0, 1)
    start_final(0)
    wait_ring(2, 0)
    start_ring(2, 1)
    wait_ring(1, 1)
    start_final(1)
    wait_ring(3, 0)
    start_ring(3, 1)
    wait_ring(2, 1)
    start_final(2)
    wait_final(0)
    wait_ring(3, 1)
    start_final(3)
    wait_final(1)

    group = lax.broadcasted_iota(jnp.int32, (16, 256), 1) >> 4
    line = lax.broadcasted_iota(jnp.int32, (16, 256), 0)

    def diagonal(full):
        total = jnp.zeros((16, 256), jnp.float32)
        for i in range(16):
            total = jnp.where(group == i, full[16 * i : 16 * i + 16], total)
        return total

    def apply(i, times):
        b, z = i >> 2, i & 3
        tail = f1[b, z].reshape(256, 640)
        x = jnp.concatenate([f0[b, z].reshape(256, 640), tail], axis=1)[:, :1200]
        for n, (g0, size) in enumerate(((0, 256), (256, 256), (512, 128), (640, 256), (896, 256), (0, 0))):
            part = times(b, x, tail, g0, size).astype(jnp.bfloat16)
            if size == 0:
                s1[b, z, :, :, :, 512:640] = part.reshape(4, 4, 16, 128)
                tt[b, z] = diagonal(lax.dot_general(tail[:, 512:], part, NT, preferred_element_type=jnp.float32))
            else:
                to, at = (s0, g0) if g0 < 640 else (s1, g0 - 640)
                to[b, z, :, :, :, at : at + size] = part.reshape(4, 4, 16, size)

    def one(which, x, g0, size):
        w = w2[which, g0 : g0 + size, :] if size else wt[which]
        return lax.dot_general(x, w, NT, preferred_element_type=jnp.float32)

    fixed = 8 if whole else 0

    @pl.loop(0, fixed)
    def _(i):
        apply(i, lambda b, x, tail, g0, size: one(core, x, g0, size))

    def either(b, x, tail, g0, size):
        flag = tail[:, 624:625].astype(jnp.float32) > 0.5
        return jnp.where(flag, one(1, x, g0, size), one(0, x, g0, size))

    @pl.loop(fixed, 4 * slots)
    def _(i):
        apply(i, either)

    wait_final(2)

    @pl.loop(0, 4 * slots)
    def _(i):
        b, z = i >> 2, i & 3
        full = lax.dot_general(
            f2[b, z].reshape(256, 640), s0[b, z].reshape(256, 640), NT, preferred_element_type=jnp.float32
        )
        tt[b, z] = tt[b, z] + diagonal(full)

    wait_final(3)

    @pl.loop(0, 4 * slots)
    def _(i):
        b, z = i >> 2, i & 3
        full = lax.dot_general(
            f3[b, z].reshape(256, 512),
            s1[b, z, :, :, :, :512].reshape(256, 512),
            NT,
            preferred_element_type=jnp.float32,
        )
        got = diagonal(full) + tt[b, z]
        turned = jnp.where(group == line, got, 0.0)
        for k in range(1, 16):
            shifted = pltpu.roll(pltpu.roll(got, 16 - k, 0), 16 * k, 1)
            turned = jnp.where(group == ((line + k) & 15), shifted, turned)
        for slot in range(16):
            zbuf[b, z, slot >> 2, slot & 3, 0:1] = turned[slot : slot + 1, :128]
            zbuf[b, z, slot >> 2, slot & 3, 1:2] = turned[slot : slot + 1, 128:]
        back_core = jnp.where(b < 2, b, core) if whole else core
        mine = (z == here[Z]) & (back_core == core)
        src = zbuf.at[b, z]
        dst = ybuf.at[:, :, jnp.where(b < 2, core, b) if whole else 0, here[Z]]

        @pl.when(mine)
        def _():
            pltpu.make_async_copy(src, dst, back_recv.at[0]).start()

        @pl.when(jnp.logical_not(mine))
        def _():
            pltpu.make_async_remote_copy(
                src, dst, back_send.at[0], back_recv.at[0],
                device_id=dev(moved(Z, z), back_core), device_id_type=MESH,
            ).start()

    pltpu.make_async_copy(ybuf, ybuf, back_recv.at[0]).wait()
    back_own = pltpu.make_async_copy(ybuf.at[here[Y], here[X]], dbuf.at[here[Y], here[X]], back_recv.at[16])
    back_own.start()

    def back(dy, dx):
        chip = across(dy, dx)
        return pltpu.make_async_remote_copy(
            ybuf.at[chip[Y], chip[X]], dbuf.at[here[Y], here[X]],
            back_send.at[4 * dy + dx], back_recv.at[4 * dy + dx],
            device_id=dev(chip, core), device_id_type=MESH,
        )

    ways = [(dy, dx) for dy in (2, 1, 3, 0) for dx in (2, 1, 3, 0) if dy or dx]
    for way in ways:
        back(*way).start()
    back_own.wait()
    for way in ways:
        back(*way).wait()

    @pl.loop(0, 4 * slots - (2 if whole else 1))
    def _(_):
        pltpu.make_async_copy(zbuf.at[0, 0], zbuf.at[0, 0], back_send.at[0]).wait()

    out_ref[...] = dbuf[...]


def direct_terms(slots, *args):
    hbm = pl.BlockSpec(memory_space=pl.ANY)
    vmem = pl.BlockSpec(memory_space=pltpu.VMEM)
    bf16, f32 = jnp.bfloat16, jnp.float32
    whole = slots == 3
    count = args[-2].shape[2]
    wide = [(slots, 4, 4, 4, 16, w) for w in WIDTHS]
    back = (4, 4, slots, 4, 2, 128)
    dma = pltpu.SemaphoreType.DMA
    shape = jax.ShapeDtypeStruct
    small = [shape(back, f32)]
    extra = []
    if whole:
        small += [
            shape((256, 128), f32), shape((256, count), bf16), shape((16, count), bf16),
            shape((1, count), jnp.int32), shape((8, TILE), f32),
        ]
        extra = [
            pltpu.VMEM((8,) + args[1].shape, bf16), pltpu.VMEM((8, 8, TILE), f32), pltpu.VMEM((16, 8, TILE), f32),
            dma((2, 8)), dma((2, 8)), dma((2, 16)),
        ]
    out = pl.pallas_call(
        functools.partial(place_kernel, slots),
        out_shape=(*small, *(shape(w, bf16) for w in wide), *(shape(w, bf16) for w in wide)),
        in_specs=[vmem, hbm, vmem, vmem, hbm, hbm, hbm] if whole else [vmem, vmem, hbm, hbm, hbm],
        out_specs=(vmem,) * len(small) + (hbm,) * 8,
        scratch_shapes=[
            pltpu.VMEM((16, 1200, count), bf16),
            pltpu.VMEM((16, 1200 - MAIN, count), bf16),
            pltpu.VMEM((2, slots, 4, 4, 16, WIDTHS[0]), bf16),
            *(pltpu.VMEM(w, bf16) for w in wide),
            *(pltpu.VMEM(w, bf16) for w in wide),
            pltpu.VMEM((2, 1200, 1200), bf16),
            pltpu.VMEM((2, TILE, 1200), bf16),
            pltpu.VMEM((slots * 64 * 16, TILE), f32),
            pltpu.VMEM((slots, 4, 16, 256), f32),
            pltpu.VMEM((slots, 4, 4, 4, 2, 128), f32),
            pltpu.VMEM(back, f32),
            pltpu.VMEM(back, f32),
            dma((4,)),
            dma((2,)),
            dma((4, 3, 3, 4)),
            dma((4, 3, 2, 4)),
            dma((4, 3, 4)),
            dma((4, 3, 3)),
            dma((4, 3, 3)),
            dma((17,)),
            dma((17,)),
            *extra,
        ],
        compiler_params=pltpu.CompilerParams(
            collective_id=slots, has_side_effects=True, vmem_limit_bytes=56 * 2**20
        ),
    )(*args)
    return (out[0].reshape(slots * 64, 256), *out[1 : len(small)])


def shards(q_index, cond_pairs, val_pairs, row_vc, col_vc, coulomb, screened):
    count = cond_pairs.shape[0]
    val_t = val_pairs.transpose(1, 2, 0)
    cond_t = cond_pairs.transpose(1, 2, 0)
    direct, exchange, onehot, flags, place, crowd = direct_terms(
        3, q_index.reshape(1, count), row_vc, col_vc, coulomb[None, :], val_t, cond_t, screened
    )

    def left(*args):
        return direct_terms(1, *args)[0]

    def none(*args):
        return jnp.zeros((64, 256), jnp.float32)

    rest = lax.cond(crowd[0, 0] > 0.5, left, none, onehot[192:], flags, val_t, cond_t, screened)
    slot, chip = place[0] & 3, place[0] >> 2
    at = jnp.where(slot < 3, ((chip >> 2) * 3 + slot) * 4 + (chip & 3), 192 + chip)
    direct = jnp.concatenate([direct, rest], axis=0)[at]
    direct = direct.reshape(count, 4, 4, 4, 4).transpose(0, 3, 1, 4, 2).reshape(count, 256)
    exchange = exchange.reshape(16, 16, 8, 16).transpose(0, 2, 1, 3).reshape(count, 256)
    return 2.0 * exchange - direct


def solution(mesh):
    return jax.shard_map(
        shards,
        mesh=mesh,
        in_specs=(
            P(("kb", "col"), None),
            P(("kb", "col"), None, None),
            P(("kb", "col"), None, None),
            P(("kb", "col"), None, None),
            P("col", None, None),
            P(),
            P(("kb", "col"), None, None),
        ),
        out_specs=P(("kb", "col"), None),
        check_vma=False,
    )
```

```python
import functools

import jax
import jax.numpy as jnp
from jax import lax
from jax.experimental import pallas as pl
from jax.experimental.pallas import tpu as pltpu
from jax.sharding import PartitionSpec as P

MESH = pl.DeviceIdType.MESH
Z, Y, X = 0, 1, 2
ORDERS = ((X, Y, Z), (Y, Z, X), (Z, X, Y))
MAIN = 1152
TILE = 128
WIDTHS = (640, 640, 640, 512)
CUTS = ((0, 256, 512, 640), (0, 128, 384, 640), (0, 256, 384, 640), (0, 128, 256, 512))
NT = (((1,), (1,)), ((), ()))


def streams(slots, r):
    out = [(j, ORDERS[j], 0, WIDTHS[r]) for j in range(3)]
    if slots == 4:
        out += [(3, ORDERS[i], CUTS[r][i], CUTS[r][i + 1]) for i in range(3)]
    return out


def at_axis(ref, lead, axis, index, c0=None, c1=None):
    where = [slice(None)] * 3
    where[axis] = index
    return ref.at[(lead, *where, slice(None), slice(c0, c1))]


def place_kernel(
    slots,
    onehot, flag_ref, rows_hbm, cols_ref, coulomb_ref, val_hbm, cond_hbm, w_hbm,
    out_ref, ex_ref, h10, h11, h12, h13, h20, h21, h22, h23,
    vt, ct, s0, s1, s2, s3, f0, f1, f2, f3, w2, wt, st, rows, tt, zbuf, ybuf, xbuf, dbuf,
    in_sem, w_sem, row_sem, send, recv, last, local, back_send, back_recv,
):
    kb = lax.axis_index("kb")
    col = lax.axis_index("col")
    here = (kb & 3, kb >> 2, col >> 1)
    core = col & 1
    count = onehot.shape[0]
    per = 64 * 16

    def dev(chip, which):
        return (chip[Y] * 4 + chip[Z], chip[X] * 2 + which)

    def moved(axis, index):
        chip = list(here)
        chip[axis] = index
        return tuple(chip)

    load_val = pltpu.make_async_copy(val_hbm, vt, in_sem.at[0])
    load_val.start()
    load_tail = pltpu.make_async_copy(cond_hbm.at[:, MAIN:], ct, in_sem.at[1])
    load_tail.start()
    load_w = pltpu.make_async_copy(w_hbm.at[0], w2.at[core], in_sem.at[2])
    load_w.start()
    load_rows = pltpu.make_async_copy(rows_hbm, rows.at[col], in_sem.at[3])
    load_rows.start()

    barrier = pltpu.get_barrier_semaphore()
    for axis in range(3):
        for d in (1, 2, 3):
            for which in range(2):
                pl.semaphore_signal(
                    barrier, inc=1, device_id=dev(moved(axis, (here[axis] + d) & 3), which), device_id_type=MESH
                )
    pl.semaphore_signal(barrier, inc=1, device_id=dev(here, 1 - core), device_id_type=MESH)

    rounds = ((s0, h10, h20, f0), (s1, h11, h21, f1), (s2, h12, h22, f2), (s3, h13, h23, f3))
    parts = tuple(streams(slots, r) for r in range(4))
    n_streams = len(parts[0])

    def fill(buf, tile, chunk_of):
        for row in range(16):
            st[pl.ds(row, count, stride=16), :] = lax.dot_general(
                onehot[...], chunk_of(row), NT, preferred_element_type=jnp.float32
            )
        for j in range(slots):
            buf[j, :, :, :, :, pl.ds(pl.multiple_of(tile * TILE, TILE), TILE)] = (
                st[j * per : (j + 1) * per].astype(jnp.bfloat16).reshape(4, 4, 4, 16, TILE)
            )

    def build(buf, first, tiles):
        @pl.loop(0, tiles)
        def _(t):
            fill(buf, t, lambda row: vt[row, pl.ds(pl.multiple_of((first + t) * TILE, TILE), TILE), :])

    def ring(r, s, k, d):
        j, order, c0, c1 = parts[r][s]
        axis = order[k]
        there = (here[axis] + d) & 3
        return pltpu.make_async_remote_copy(
            at_axis(rounds[r][k], j, axis, there, c0, c1),
            at_axis(rounds[r][k + 1], j, axis, here[axis], c0, c1),
            send.at[r, s, k, d], recv.at[r, s, k, d],
            device_id=dev(moved(axis, there), core), device_id_type=MESH,
        )

    def keep(r, s, k):
        j, order, c0, c1 = parts[r][s]
        axis = order[k]
        return pltpu.make_async_copy(
            at_axis(rounds[r][k], j, axis, here[axis], c0, c1),
            at_axis(rounds[r][k + 1], j, axis, here[axis], c0, c1),
            local.at[r, s, k],
        )

    def start_ring(r, k):
        for d in (1, 3, 2):
            for s in range(n_streams):
                ring(r, s, k, d).start()
        for s in range(n_streams):
            keep(r, s, k).start()

    def wait_ring(r, k):
        for s in range(n_streams):
            for d in (1, 3, 2):
                c = ring(r, s, k, d)
                c.wait_send()
                c.wait_recv()
            keep(r, s, k).wait()

    def final(r, s, d):
        j, order, c0, c1 = parts[r][s]
        axis = order[2]
        there = (here[axis] + d) & 3
        lead, goal = (core, j) if j < 2 else (j, core)
        sem = last.at[r, lead, d] if j < 2 else last.at[r, s, d]
        return pltpu.make_async_remote_copy(
            at_axis(rounds[r][2], j, axis, there, c0, c1),
            at_axis(rounds[r][3], lead, axis, here[axis], c0, c1),
            send.at[r, s, 2, d], sem,
            device_id=dev(moved(axis, there), goal), device_id_type=MESH,
        )

    def final_local(r, s):
        j, order, c0, c1 = parts[r][s]
        axis = order[2]
        lead = core if j < 2 else j
        return pltpu.make_async_copy(
            at_axis(rounds[r][2], j, axis, here[axis], c0, c1),
            at_axis(rounds[r][3], lead, axis, here[axis], c0, c1),
            local.at[r, s, 2],
        )

    def start_final(r):
        for d in (1, 3, 2):
            for s in range(n_streams):
                final(r, s, d).start()
        for s in range(n_streams):
            if s < 2:
                @pl.when(core == s)
                def _():
                    final_local(r, s).start()

                @pl.when(core != s)
                def _():
                    final(r, s, 0).start()
            else:
                final_local(r, s).start()

    def wait_final(r):
        for s in range(n_streams):
            for d in (1, 3, 2):
                final(r, s, d).wait_send()
            if s < 2:
                @pl.when(core == s)
                def _():
                    final_local(r, s).wait()

                @pl.when(core != s)
                def _():
                    final(r, s, 0).wait_send()
            else:
                final_local(r, s).wait()
                for d in (1, 3, 2):
                    final(r, s, d).wait_recv()
        for mine in range(2):
            axis = ORDERS[mine][2]

            @pl.when(core == mine)
            def _():
                for lead in range(2):
                    for d in (1, 3, 2) if lead == mine else (1, 3, 2, 0):
                        at = at_axis(rounds[r][3], lead, axis, here[axis])
                        pltpu.make_async_remote_copy(
                            at, at, send.at[r, mine, 2, d], last.at[r, lead, d],
                            device_id=dev(here, 1 - core), device_id_type=MESH,
                        ).wait_recv()

    pl.semaphore_wait(barrier, 19)
    def row_copy(d):
        to = lax.rem(col + d, 8)
        return pltpu.make_async_remote_copy(
            rows_hbm, rows.at[col], row_sem.at[0, d], row_sem.at[1, d], device_id=(kb, to), device_id_type=MESH
        )

    for d in range(1, 8):
        row_copy(d).start()

    load_val.wait()
    build(s0, 0, 5)
    start_ring(0, 0)
    load_tail.wait()
    build(s1, 5, 4)
    gap = jnp.zeros((16, TILE), jnp.bfloat16)
    fill(s1, 4, lambda row: jnp.concatenate([vt[row, MAIN:, :], gap, ct[row], flag_ref[...]], axis=0))
    load_cond = pltpu.make_async_copy(cond_hbm, vt, in_sem.at[0])
    load_cond.start()
    start_ring(1, 0)

    send_w = pltpu.make_async_remote_copy(
        w_hbm.at[0], w2.at[core], w_sem.at[0], w_sem.at[1], device_id=dev(here, 1 - core), device_id_type=MESH
    )
    send_w.start()

    load_cond.wait()
    build(s2, 0, 5)
    wait_ring(0, 0)
    start_ring(0, 1)
    start_ring(2, 0)
    build(s3, 5, 4)
    wait_ring(1, 0)
    start_ring(1, 1)
    start_ring(3, 0)

    load_rows.wait()
    for d in range(1, 8):
        row_copy(d).wait()
    scaled = (cols_ref[...].astype(jnp.float32) * coulomb_ref[...][None]).astype(jnp.bfloat16)
    ex_ref[...] = lax.dot_general(
        rows[...].reshape(256, 1200), scaled.reshape(128, 1200), NT, preferred_element_type=jnp.float32
    )
    load_w.wait()
    send_w.wait()
    wt[...] = jnp.zeros_like(wt)
    for which in range(2):
        wt[which, 64:112] = w2[which, MAIN:]

    wait_ring(0, 1)
    start_final(0)
    wait_ring(2, 0)
    start_ring(2, 1)
    wait_ring(1, 1)
    start_final(1)
    wait_ring(3, 0)
    start_ring(3, 1)
    wait_ring(2, 1)
    start_final(2)
    wait_final(0)
    wait_ring(3, 1)
    start_final(3)
    wait_final(1)

    group = lax.broadcasted_iota(jnp.int32, (16, 256), 1) >> 4
    line = lax.broadcasted_iota(jnp.int32, (16, 256), 0)

    def diagonal(full):
        total = jnp.zeros((16, 256), jnp.float32)
        for i in range(16):
            total = jnp.where(group == i, full[16 * i : 16 * i + 16], total)
        return total

    def apply(i, times):
        b, z = i >> 2, i & 3
        tail = f1[b, z].reshape(256, 640)
        x = jnp.concatenate([f0[b, z].reshape(256, 640), tail], axis=1)[:, :1200]
        for n, (g0, size) in enumerate(((0, 256), (256, 256), (512, 128), (640, 256), (896, 256), (0, 0))):
            part = times(b, x, tail, g0, size).astype(jnp.bfloat16)
            if size == 0:
                s1[b, z, :, :, :, 512:640] = part.reshape(4, 4, 16, 128)
                tt[b, z] = diagonal(lax.dot_general(tail[:, 512:], part, NT, preferred_element_type=jnp.float32))
            else:
                to, at = (s0, g0) if g0 < 640 else (s1, g0 - 640)
                to[b, z, :, :, :, at : at + size] = part.reshape(4, 4, 16, size)

    def one(which, x, g0, size):
        w = w2[which, g0 : g0 + size, :] if size else wt[which]
        return lax.dot_general(x, w, NT, preferred_element_type=jnp.float32)

    fixed = 8 if slots == 3 else 16

    @pl.loop(0, fixed)
    def _(i):
        apply(i, lambda b, x, tail, g0, size: one(jnp.where(b < 2, core, b - 2), x, g0, size))

    if slots == 3:
        def either(b, x, tail, g0, size):
            flag = tail[:, 624:625].astype(jnp.float32) > 0.5
            return jnp.where(flag, one(1, x, g0, size), one(0, x, g0, size))

        @pl.loop(8, 12)
        def _(i):
            apply(i, either)

    wait_final(2)

    @pl.loop(0, 4 * slots)
    def _(i):
        b, z = i >> 2, i & 3
        full = lax.dot_general(
            f2[b, z].reshape(256, 640), s0[b, z].reshape(256, 640), NT, preferred_element_type=jnp.float32
        )
        tt[b, z] = tt[b, z] + diagonal(full)

    wait_final(3)

    @pl.loop(0, 4 * slots)
    def _(i):
        b, z = i >> 2, i & 3
        full = lax.dot_general(
            f3[b, z].reshape(256, 512),
            s1[b, z, :, :, :, :512].reshape(256, 512),
            NT,
            preferred_element_type=jnp.float32,
        )
        got = diagonal(full) + tt[b, z]
        turned = jnp.where(group == line, got, 0.0)
        for k in range(1, 16):
            shifted = pltpu.roll(pltpu.roll(got, 16 - k, 0), 16 * k, 1)
            turned = jnp.where(group == ((line + k) & 15), shifted, turned)
        for slot in range(16):
            zbuf[b, z, slot >> 2, slot & 3, 0:1] = turned[slot : slot + 1, :128]
            zbuf[b, z, slot >> 2, slot & 3, 1:2] = turned[slot : slot + 1, 128:]
        back_core = jnp.where(b < 2, b, core)
        mine = (z == here[Z]) & (back_core == core)
        src = zbuf.at[b, z]
        dst = ybuf.at[jnp.where(b < 2, core, b), here[Z]]

        @pl.when(mine)
        def _():
            pltpu.make_async_copy(src, dst, back_recv.at[0]).start()

        @pl.when(jnp.logical_not(mine))
        def _():
            pltpu.make_async_remote_copy(
                src, dst, back_send.at[0], back_recv.at[0],
                device_id=dev(moved(Z, z), back_core), device_id_type=MESH,
            ).start()

    pltpu.make_async_copy(ybuf, ybuf, back_recv.at[0]).wait()

    def back(j, k, d):
        axis = ((Y, X) if j < 2 else (X, Y))[k]
        src, dst = ((ybuf, xbuf), (xbuf, dbuf))[k]
        there = (here[axis] + d) & 3
        return pltpu.make_async_remote_copy(
            at_axis(src, j, axis, there), at_axis(dst, j, axis, here[axis]),
            back_send.at[1 + 16 * k + 4 * j + d], back_recv.at[1 + 16 * k + 4 * j + d],
            device_id=dev(moved(axis, there), core), device_id_type=MESH,
        )

    def back_keep(j, k):
        axis = ((Y, X) if j < 2 else (X, Y))[k]
        src, dst = ((ybuf, xbuf), (xbuf, dbuf))[k]
        return pltpu.make_async_copy(
            at_axis(src, j, axis, here[axis]), at_axis(dst, j, axis, here[axis]), back_recv.at[1 + 16 * k + 4 * j]
        )

    for k in range(2):
        for d in (2, 1, 3):
            for j in range(slots):
                back(j, k, d).start()
        for j in range(slots):
            back_keep(j, k).start()
        for j in range(slots):
            back_keep(j, k).wait()
            for d in (1, 3, 2):
                back(j, k, d).wait()

    @pl.loop(0, 4 * slots - (slots - 1))
    def _(_):
        pltpu.make_async_copy(zbuf.at[0, 0], zbuf.at[0, 0], back_send.at[0]).wait()

    out_ref[...] = dbuf[...]


def direct_terms(slots, onehot, flags, row_vc, col_vc, coulomb, val_t, cond_t, screened):
    hbm = pl.BlockSpec(memory_space=pl.ANY)
    vmem = pl.BlockSpec(memory_space=pltpu.VMEM)
    bf16 = jnp.bfloat16
    wide = [(slots, 4, 4, 4, 16, w) for w in WIDTHS]
    small = (slots, 4, 4, 4, 2, 128)
    f32 = jnp.float32
    dma = pltpu.SemaphoreType.DMA
    out = pl.pallas_call(
        functools.partial(place_kernel, slots),
        out_shape=(
            jax.ShapeDtypeStruct(small, f32),
            jax.ShapeDtypeStruct((256, 128), f32),
            *(jax.ShapeDtypeStruct(w, bf16) for w in wide),
            *(jax.ShapeDtypeStruct(w, bf16) for w in wide),
        ),
        in_specs=[vmem, vmem, hbm, vmem, vmem, hbm, hbm, hbm],
        out_specs=(vmem, vmem) + (hbm,) * 8,
        scratch_shapes=[
            pltpu.VMEM(val_t.shape, bf16),
            pltpu.VMEM((16, 48, 128), bf16),
            *(pltpu.VMEM(w, bf16) for w in wide),
            *(pltpu.VMEM(w, bf16) for w in wide),
            pltpu.VMEM((2, 1200, 1200), bf16),
            pltpu.VMEM((2, TILE, 1200), bf16),
            pltpu.VMEM((slots * 64 * 16, TILE), f32),
            pltpu.VMEM((8, 2, 16, 1200), bf16),
            pltpu.VMEM((slots, 4, 16, 256), f32),
            *(pltpu.VMEM(small, f32) for _ in range(4)),
            dma((4,)),
            dma((2,)),
            dma((2, 8)),
            dma((4, 6, 3, 4)),
            dma((4, 6, 2, 4)),
            dma((4, 6, 4)),
            dma((4, 6, 3)),
            dma((33,)),
            dma((33,)),
        ],
        compiler_params=pltpu.CompilerParams(
            collective_id=slots, has_side_effects=True, vmem_limit_bytes=61 * 2**20
        ),
    )(onehot, flags, row_vc, col_vc, coulomb, val_t, cond_t, screened)
    return out[0].reshape(slots * 64, 256), out[1]


def shards(q_index, cond_pairs, val_pairs, row_vc, col_vc, coulomb, screened):
    count = cond_pairs.shape[0]
    slots = 4
    target = q_index[:, 0]
    same = target[:, None] == target[None, :]
    earlier = jnp.arange(count)[None, :] < jnp.arange(count)[:, None]
    rank = jnp.sum((same & earlier).astype(jnp.int32), axis=1)
    core, x, z, y = target & 1, (target >> 1) & 3, (target >> 3) & 3, (target >> 5) & 3
    chip = (z * 4 + y) * 4 + x
    place = (rank * 2 + core) * 64 + chip
    spots = jnp.arange(slots * 64, dtype=jnp.int32)
    onehot = (place[None, :] == spots[:, None]).astype(jnp.bfloat16)
    flags = jnp.broadcast_to(core.astype(jnp.bfloat16)[None, :], (16, count))
    direct, exchange = direct_terms(
        slots, onehot, flags, row_vc, col_vc, coulomb[None, :],
        val_pairs.transpose(1, 2, 0), cond_pairs.transpose(1, 2, 0), screened,
    )
    direct = direct[place].reshape(count, 4, 4, 4, 4).transpose(0, 3, 1, 4, 2).reshape(count, 256)
    exchange = exchange.reshape(16, 16, 8, 16).transpose(0, 2, 1, 3).reshape(count, 256)
    return 2.0 * exchange - direct


def solution(mesh):
    return jax.shard_map(
        shards,
        mesh=mesh,
        in_specs=(
            P(("kb", "col"), None),
            P(("kb", "col"), None, None),
            P(("kb", "col"), None, None),
            P(("kb", "col"), None, None),
            P("col", None, None),
            P(),
            P(("kb", "col"), None, None),
        ),
        out_specs=P(("kb", "col"), None),
        check_vma=False,
    )
```
